32 devices in a mesh: parts: 2 (over x), route: 16 (over z, y, core).
Axes of the slice: x: 2, y: 2, z: 4, core: 2. Of those that a mesh axis runs over, the one named last changes fastest.
Arguments:
- codes: float32 [16384, 256], P(('parts', 'route')), parts along dimension 0, may hold values from -256 to 256
- labels: int32 [16384], P(('parts', 'route')), parts along dimension 0, may hold values from 0 to 31, as said below
- centroids: bfloat16 [64, 1024, 256], P(('parts', 'route')), parts along dimension 0, may hold values from -6 to 6
- sharpness: bfloat16 [64], P(('parts', 'route')), parts along dimension 0, may hold values from 0.04 to 0.1
Outputs:
- soft_labels: bfloat16 [16384, 1024], P(('parts', 'route')), parts along dimension 0
- new_centroids: float32 [64, 1024, 256], P(('parts', 'route')), parts along dimension 0
The draws below stay inside these ranges and needn't reach their ends.
There are 2 independent parts, one for each index of `parts`. The reference program is written for one: setup_inputs(seed, part) draws one part's arguments, and reference() takes and returns one part's arrays. A program takes and returns all parts, laid end to end along the dimension named above; each array names one. Nothing has to cross between parts.
Inputs may be any that keep to these rules, and one draw needn't show every extreme that they name: Counting frames from 0 within each device, frame i is handled by the device of index 4 * (labels // 8) + i mod 4; cluster c belongs to the device of index c // 2. At most 64 frames of one device are handled by any one device, and in every draw some 4 devices each handle exactly 64 frames of every device.
All inputs are finite; a program needn't handle non-finite values.
Results may differ from the reference program's by a relative error of at most 0.007.
Values may be sent and summed in bfloat16 or wider, within the bound.
No kernel may reach another device: no remote copies, remote signals or barrier semaphores. Data moves between devices by JAX's collectives and lax.ppermute only.
A program may use at most 128 MiB of HBM per device.

```python
import jax
import jax.numpy as jnp
from jax import lax

DIM = 256
FINE = 1024
GRP = 4
CL_DEV = 2
F_DEV = 512
COARSE = 32
TOTAL = 8192
CAP = 64
N_ROUTE = 16


def routing_table(key):
    key = jax.random.fold_in(key, 101)
    hot_key, score_key, order_key, pick_key = jax.random.split(key, 4)
    group_count = N_ROUTE // GRP
    per_class = group_count * CAP
    take_count = F_DEV // GRP
    hot_group = jax.random.randint(hot_key, (), 0, group_count)
    candidates = jnp.arange(per_class, dtype=jnp.int32)
    noise_vals = jax.random.randint(score_key, (N_ROUTE, GRP, per_class), 0, 4096)
    scores = (noise_vals + 4096 * (candidates // CAP == hot_group).astype(jnp.int32)) * per_class + candidates
    chosen = lax.top_k(scores, take_count)[1]
    shuffle = jax.random.randint(order_key, (N_ROUTE, GRP, take_count), 0, 4096) * take_count + jnp.arange(take_count, dtype=jnp.int32)
    chosen = jnp.take_along_axis(chosen, jnp.argsort(shuffle, axis=-1), axis=-1)
    pick_vals = jax.random.randint(pick_key, (2, N_ROUTE, GRP, take_count), 0, GRP * CL_DEV)
    inner_index = jnp.minimum(pick_vals[0], pick_vals[1])
    label_grid = chosen // CAP * (GRP * CL_DEV) + inner_index
    return jnp.transpose(label_grid, (0, 2, 1)).reshape(N_ROUTE * F_DEV).astype(jnp.int32)


def first_rows(key):
    key = jax.random.fold_in(key, 202)
    return jnp.clip(jax.random.normal(key, (COARSE, DIM), jnp.float32), -6.0, 6.0)


def sharp_table(key):
    key = jax.random.fold_in(key, 301)
    return jnp.exp(jax.random.uniform(key, (COARSE,), jnp.float32, jnp.log(0.04), jnp.log(0.1)))


def draw_labels(key, part):
    table = routing_table(key)
    return table


def draw_sharpness(key, part):
    table = sharp_table(key)
    return table.astype(jnp.bfloat16)


def draw_centroids(key, part):
    first_row = first_rows(key)
    key = jax.random.fold_in(key, 3)
    other_rows = jnp.clip(jax.random.normal(key, (COARSE, FINE - 1, DIM), jnp.float32), -6.0, 6.0)
    return jnp.concatenate([first_row[:, None, :], other_rows], axis=1).astype(jnp.bfloat16)


def draw_codes(key, part):
    key = jax.random.fold_in(key, 4)
    main_key = jax.random.fold_in(key, 0)
    code_vals = jnp.clip(jax.random.normal(main_key, (TOTAL, DIM), jnp.float32), -6.0, 6.0)
    return jnp.clip(code_vals, -256.0, 256.0)


def setup_inputs(seed: int = 0, part: int = 0) -> dict:
    arg_keys = jax.random.split(jax.random.key(seed), 5)
    part_splits = jax.random.split(jax.random.fold_in(arg_keys[4], part), 5)
    return {
        "codes": draw_codes(jax.random.fold_in(jax.random.fold_in(arg_keys[4], part), 71), part),
        "labels": draw_labels(jax.random.fold_in(jax.random.fold_in(arg_keys[4], part), 71), part),
        "centroids": draw_centroids(jax.random.fold_in(jax.random.fold_in(arg_keys[4], part), 71), part),
        "sharpness": draw_sharpness(jax.random.fold_in(jax.random.fold_in(arg_keys[4], part), 71), part),
    }


def reference(codes, labels, centroids, sharpness):
    row_count = F_DEV * N_ROUTE
    block_size = 128
    rounded = codes.astype(jnp.bfloat16)
    cent_wide = centroids.astype(jnp.float32)
    half_norm = 0.5 * jnp.einsum("kfd,kfd->kf", cent_wide, cent_wide)
    scale_vals = sharpness.astype(jnp.float32)
    order = jnp.argsort(labels, stable=True).astype(jnp.int32)
    counts = jax.ops.segment_sum(jnp.ones((row_count,), jnp.int32), labels, num_segments=COARSE)
    first = jnp.cumsum(counts) - counts
    padded = (counts + block_size - 1) // block_size * block_size
    seg_ends = jnp.cumsum(padded)
    starts = seg_ends - padded
    sorted_labels = labels[order]
    slot_index = starts[sorted_labels] + jnp.arange(row_count, dtype=jnp.int32) - first[sorted_labels]
    block_count = -(-row_count // block_size) + COARSE
    frame_at = jnp.full((block_count * block_size,), -1, jnp.int32).at[slot_index].set(order)
    block_start = jnp.arange(block_count, dtype=jnp.int32) * block_size
    owners = jnp.minimum(jnp.sum((seg_ends[None, :] <= block_start[:, None]).astype(jnp.int32), axis=1), COARSE - 1)
    used_blocks = (seg_ends[-1] // block_size).astype(jnp.int32)

    def advance(block_index, state_in):
        weighted, mass_sum, soft_out = state_in
        cluster_id = owners[block_index]
        frame_ids = lax.dynamic_slice_in_dim(frame_at, block_index * block_size, block_size, 0)
        live_mask = frame_ids >= 0
        block_codes = jnp.take(rounded, jnp.maximum(frame_ids, 0), axis=0)
        centre = centroids[cluster_id]
        dot_terms = jnp.dot(block_codes, centre.T, preferred_element_type=jnp.float32)
        logits = scale_vals[cluster_id] * (dot_terms - half_norm[cluster_id][None, :])
        shifted = jnp.exp(logits - jnp.max(logits, axis=1, keepdims=True))
        soft_vals = (float(FINE) * shifted / jnp.sum(shifted, axis=1, keepdims=True)).astype(jnp.bfloat16)
        masked = soft_vals * live_mask[:, None].astype(jnp.bfloat16)
        weighted = weighted.at[cluster_id].add(jnp.dot(masked.T, block_codes, preferred_element_type=jnp.float32))
        mass_sum = mass_sum.at[cluster_id].add(jnp.sum(masked.astype(jnp.float32), axis=0))
        target_rows = jnp.where(live_mask, frame_ids, row_count)
        soft_out = soft_out.at[target_rows].set(soft_vals, mode="drop")
        return weighted, mass_sum, soft_out

    start_state = (jnp.zeros((COARSE, FINE, DIM), jnp.float32), jnp.zeros((COARSE, FINE), jnp.float32), jnp.zeros((row_count, FINE), jnp.bfloat16))
    weighted, mass_sum, soft_out = lax.fori_loop(jnp.int32(0), used_blocks, advance, start_state)
    new_centroids = (weighted + cent_wide) / (mass_sum[:, :, None] + 1.0)
    return soft_out, new_centroids
```

```python
import functools

import jax
import jax.numpy as jnp
from jax import lax
from jax.experimental import pallas as pl
from jax.experimental.pallas import tpu as pltpu
from jax.sharding import PartitionSpec as P

GRP = 4
META = 16
BF = jnp.bfloat16
F32 = jnp.float32
VMEM = pl.BlockSpec(memory_space=pltpu.VMEM)
SMEM = pl.BlockSpec(memory_space=pltpu.SMEM)


def call(body, out_shape, n_in, flops, nbytes, in_specs=None, scratch=()):
    many = isinstance(out_shape, (list, tuple))
    return pl.pallas_call(
        body,
        out_shape=out_shape,
        in_specs=in_specs or [VMEM] * n_in,
        out_specs=[VMEM] * len(out_shape) if many else VMEM,
        scratch_shapes=list(scratch),
        compiler_params=pltpu.CompilerParams(vmem_limit_bytes=40 * 1024 * 1024),
        cost_estimate=pl.CostEstimate(flops=flops, bytes_accessed=nbytes, transcendentals=0),
    )


def three(value):
    first = value.astype(BF)
    rest = value - first.astype(F32)
    second = rest.astype(BF)
    third = (rest - second.astype(F32)).astype(BF)
    return first, second, third


def cluster_lanes(shape):
    lane = lax.broadcasted_iota(jnp.int32, shape, 1)
    part = lane & 15
    pair = (lane >> 4) & 3
    norm = (lane < 64) & (part < 6)
    sharp = (lane >= 64) & (lane < 128) & ((part == 6) | (part == 7))
    plain = (lane >= 128) & (lane < 128 + 2 * GRP)
    cluster = jnp.where(
        plain,
        lane - 128,
        2 * pair + jnp.where(norm, (part >= 3).astype(jnp.int32), (part == 7).astype(jnp.int32)),
    )
    return cluster, norm | sharp | plain


def pack_body(groups, rows, key_row, key_col, codes, *outs):
    frames, width = codes.shape
    kr, kc = key_row[...], key_col[...]
    lane = lax.broadcasted_iota(jnp.int32, (1, frames), 1)
    sub = lax.broadcasted_iota(jnp.int32, (frames, 1), 0)
    ur, uc = kr * frames + lane, kc * frames + sub
    gr = kr >> 3
    base_r = gr * (8 * frames)
    rank = jnp.sum(((uc < ur) & (uc >= base_r)).astype(jnp.int32), axis=0, keepdims=True)
    slot = gr * rows + rank
    rounded = codes[...].astype(BF)
    place = lax.broadcasted_iota(jnp.int32, (rows, frames), 0)
    cluster, used = cluster_lanes((1, width))
    row = lax.broadcasted_iota(jnp.int32, (META, width), 0)
    for k in range(groups):
        pick = (slot == place + k * rows).astype(F32).astype(BF)
        outs[k][:rows, :] = jnp.dot(pick, rounded, preferred_element_type=F32).astype(BF)
        inside = kc >= 8 * k
        first = jnp.sum((inside & (kc < 8 * k + cluster)).astype(F32), axis=0, keepdims=True)
        last = jnp.sum((inside & (kc < 8 * k + cluster + 1)).astype(F32), axis=0, keepdims=True)
        last = jnp.where(used, last, first)
        bounds = jnp.where(row == 0, first, jnp.where(row == 1, last, 0.0))
        outs[k][rows:, :] = bounds.astype(BF)
    gc = kc >> 3
    base_c = gc * (8 * frames)
    rank_c = jnp.sum(((ur < uc) & (ur >= base_c)).astype(jnp.int32), axis=1, keepdims=True)
    outs[groups][...] = gc * rows + rank_c


def norm_body(sharp, centres, out):
    row = lax.broadcasted_iota(jnp.int32, (META, centres.shape[1]), 0)
    ones = jnp.ones((8, centres.shape[2]), BF)
    total = jnp.zeros(row.shape, F32)
    for c in range(centres.shape[0]):
        wide = centres[c].astype(F32)
        square = wide * wide
        high = square.astype(BF)
        low = (square - high.astype(F32)).astype(BF)
        dims = (((1,), (1,)), ((), ()))
        norm = lax.dot_general(ones, high, dims, preferred_element_type=F32)
        norm = norm + lax.dot_general(ones, low, dims, preferred_element_type=F32)
        terms = three(-0.5 * norm[0:1, :])
        for t in range(3):
            total = jnp.where(row == 3 * c + t, terms[t].astype(F32), total)
        total = jnp.where(row == 6 + c, sharp[c], total)
    out[...] = total.astype(BF)


def member_lanes(block, rows):
    bounds = block[rows:, :].astype(F32)
    row = lax.broadcasted_iota(jnp.int32, (rows, block.shape[1]), 0).astype(F32)
    return ((row >= bounds[0:1, :]) & (row < bounds[1:2, :])).astype(F32)


def soft_body(rows, block, c0, c1, c2, c3, m0, m1, m2, m3, out):
    centres = (c0, c1, c2, c3)
    member = member_lanes(block, rows)
    member_bf = member.astype(BF)
    table = jnp.concatenate([m0[...], m1[...], m2[...], m3[...]], axis=0)
    codes = block[:rows, :]
    logits = jnp.dot(member_bf[:, :64], table, preferred_element_type=F32)
    for r in range(2 * GRP):
        chosen = codes * member_bf[:, 128 + r : 129 + r]
        logits = logits + lax.dot_general(
            chosen, centres[r // 2][r % 2], (((1,), (1,)), ((), ())), preferred_element_type=F32
        )
    scale = jnp.dot(member_bf[:, 64:128], table[:, :128], preferred_element_type=F32)
    logits = logits * scale[:, 0:1]
    shifted = jnp.exp(logits - jnp.max(logits, axis=1, keepdims=True))
    fine = float(out.shape[1])
    out[...] = (shifted * (fine / jnp.sum(shifted, axis=1, keepdims=True))).astype(BF)


def weighted_body(groups, rows, which, *refs):
    blocks, softs, out = refs[:groups], refs[groups : 2 * groups], refs[2 * groups]
    width = blocks[0].shape[1]
    dims = (((0,), (0,)), ((), ()))
    members = [member_lanes(b, rows).astype(BF) for b in blocks]
    mass = 0.0
    for m, s in zip(members, softs):
        mass = mass + lax.dot_general(m[:, 128:], s[...], dims, preferred_element_type=F32)
    row = lax.broadcasted_iota(jnp.int32, (META, out.shape[2]), 0)
    for n, r in enumerate(which):
        total = 0.0
        for b, m, s in zip(blocks, members, softs):
            chosen = b[:rows, :] * m[:, 128 + r : 129 + r]
            total = total + lax.dot_general(chosen, s[...], dims, preferred_element_type=F32)
        out[n, :width, :] = total.astype(BF)
        out[n, width:, :] = mass_rows(row, mass[r : r + 1, :])


def mass_rows(row, mass):
    terms = three(mass)
    total = jnp.zeros(row.shape, F32)
    for t in range(3):
        total = jnp.where(row == t, terms[t].astype(F32), total)
    return total.astype(BF)


def combine_body(keep, got, out):
    width = out.shape[1] - META
    row = lax.broadcasted_iota(jnp.int32, (META, out.shape[2]), 0)
    for c in range(out.shape[0]):
        n = c + out.shape[0]
        out[c, :width, :] = (
            keep[n, :width, :].astype(F32) + got[n, :width, :].astype(F32)
        ).astype(BF)
        mass = keep[n, width:, :].astype(F32) + got[n, width:, :].astype(F32)
        out[c, width:, :] = mass_rows(row, jnp.sum(mass, axis=0, keepdims=True))


def finish_body(keep, got, far, centres, out):
    width = centres.shape[2]
    for c in range(out.shape[0]):
        total = keep[c].astype(F32) + got[c].astype(F32) + far[c].astype(F32)
        mass = jnp.sum(total[width:, :], axis=0, keepdims=True) + 1.0
        column = jnp.broadcast_to(mass, (8, mass.shape[1])).T[:, 0:1]
        out[c] = (total[:width, :].T + centres[c].astype(F32)) / column


def unpack_body(groups, rows, slot, *refs):
    frames = slot.shape[0]
    out = refs[groups]
    lane = lax.broadcasted_iota(jnp.int32, (frames, rows), 1)
    total = 0.0
    for k in range(groups):
        pick = (slot[...] == lane + k * rows).astype(F32).astype(BF)
        total = total + jnp.dot(pick, refs[k][...], preferred_element_type=F32)
    out[...] = total.astype(BF)


def shards(codes, labels, centroids, sharpness):
    route = lax.axis_size("route")
    frames, width = codes.shape
    per_device, fine, _ = centroids.shape
    groups = route // GRP
    rows = GRP * max(8, 2 * frames // route)
    me = lax.axis_index("route")
    group, place = me // GRP, me % GRP

    def swap(x, mask):
        return lax.ppermute(x, "route", [(r, r ^ mask) for r in range(route)])

    within = labels % (GRP * per_device)
    key = ((labels // (GRP * per_device)) ^ group) * (GRP * per_device) + (
        ((within // per_device) ^ place) * per_device + within % per_device
    )
    far_centres = swap(centroids, 2)
    block_shape = jax.ShapeDtypeStruct((rows + META, width), BF)
    *send, slot = call(
        functools.partial(pack_body, groups, rows),
        [block_shape] * groups + [jax.ShapeDtypeStruct((frames, 1), jnp.int32)],
        3,
        2 * groups * rows * frames * width,
        frames * width * 8,
    )(key.reshape(1, frames), key.reshape(frames, 1), codes)
    order = sorted(range(1, groups), key=lambda k: (-(k.bit_length()), k))
    blocks = {0: send[0]}
    for k in order:
        blocks[k] = swap(send[k], GRP * k)
    near_centres = swap(centroids, 1)
    meta = call(
        norm_body,
        jax.ShapeDtypeStruct((META, fine), BF),
        2,
        4 * 8 * per_device * fine * width,
        per_device * fine * width * 2,
        in_specs=[SMEM, VMEM],
    )(sharpness.astype(F32), centroids)
    metas = [meta] + [swap(meta, m) for m in range(1, GRP)]
    last_centres = swap(far_centres, 1)

    soft = {}
    back = {}
    for k in order + [0]:
        soft[k] = call(
            functools.partial(soft_body, rows),
            jax.ShapeDtypeStruct((rows, fine), BF),
            9,
            2 * rows * fine * width * 2 * GRP,
            GRP * per_device * fine * width * 2,
        )(blocks[k], centroids, near_centres, far_centres, last_centres, *metas)
        back[k] = swap(soft[k], GRP * k) if k else soft[k]

    def sums(which):
        return call(
            functools.partial(weighted_body, groups, rows, which),
            jax.ShapeDtypeStruct((len(which), width + META, fine), BF),
            2 * groups,
            2 * groups * rows * fine * width * len(which),
            groups * rows * fine * 2,
        )(*[blocks[k] for k in range(groups)], *[soft[k] for k in range(groups)])

    got = swap(sums((2, 3, 6, 7)), 1)
    keep = sums((0, 1, 4, 5))
    chip = call(
        combine_body,
        jax.ShapeDtypeStruct((per_device, width + META, fine), BF),
        2,
        per_device * fine * width * 4,
        per_device * fine * width * 12,
    )(keep, got)
    far = swap(chip, 2)
    new_centroids = call(
        finish_body,
        jax.ShapeDtypeStruct(centroids.shape, F32),
        4,
        per_device * fine * width * 8,
        per_device * fine * width * 16,
    )(keep, got, far, centroids)
    soft_labels = call(
        functools.partial(unpack_body, groups, rows),
        jax.ShapeDtypeStruct((frames, fine), BF),
        1 + groups,
        2 * frames * groups * rows * fine,
        groups * rows * fine * 2,
    )(slot, *[back[k] for k in range(groups)])
    return soft_labels, new_centroids


def solution(mesh):
    placed = (
        P(("parts", "route"), None),
        P(("parts", "route")),
        P(("parts", "route"), None, None),
        P(("parts", "route")),
    )
    return jax.shard_map(
        shards,
        mesh=mesh,
        in_specs=placed,
        out_specs=(P(("parts", "route"), None), P(("parts", "route"), None, None)),
        check_vma=False,
    )
```

```python
import functools

import jax
import jax.numpy as jnp
from jax import lax
from jax.experimental import pallas as pl
from jax.experimental.pallas import tpu as pltpu
from jax.sharding import PartitionSpec as P

GRP = 4
META = 16
SCALE = 5
BF = jnp.bfloat16
F32 = jnp.float32
VMEM = pl.BlockSpec(memory_space=pltpu.VMEM)
SMEM = pl.BlockSpec(memory_space=pltpu.SMEM)


def call(body, out_shape, n_in, flops, nbytes, in_specs=None, scratch=()):
    many = isinstance(out_shape, (list, tuple))
    return pl.pallas_call(
        body,
        out_shape=out_shape,
        in_specs=in_specs or [VMEM] * n_in,
        out_specs=[VMEM] * len(out_shape) if many else VMEM,
        scratch_shapes=list(scratch),
        compiler_params=pltpu.CompilerParams(vmem_limit_bytes=40 * 1024 * 1024),
        cost_estimate=pl.CostEstimate(flops=flops, bytes_accessed=nbytes, transcendentals=0),
    )


def three(value):
    first = value.astype(BF)
    rest = value - first.astype(F32)
    second = rest.astype(BF)
    third = (rest - second.astype(F32)).astype(BF)
    return first, second, third


def cluster_lanes(shape):
    lane = lax.broadcasted_iota(jnp.int32, shape, 1)
    return jnp.where(lane < 128, lane >> 4, lane - 128)


def pack_body(groups, rows, here, labels, codes, *outs):
    frames, width = codes.shape
    group, place = here[0] // GRP, here[0] % GRP
    kr = jnp.broadcast_to(labels[...], (8, frames)) ^ (group * 8 + place * 2)
    kc = kr.T[:, 0:1]
    kr = kr[0:1, :]
    lane = lax.broadcasted_iota(jnp.int32, (1, frames), 1)
    sub = lax.broadcasted_iota(jnp.int32, (frames, 1), 0)
    ur, uc = kr * frames + lane, kc * frames + sub
    gr = kr >> 3
    base_r = gr * (8 * frames)
    rank = jnp.sum(((uc < ur) & (uc >= base_r)).astype(jnp.int32), axis=0, keepdims=True)
    slot = gr * rows + rank
    rounded = codes[...].astype(BF)
    target = lax.broadcasted_iota(jnp.int32, (rows, frames), 0)
    cluster = cluster_lanes((1, width))
    row = lax.broadcasted_iota(jnp.int32, (META, width), 0)
    for k in range(groups):
        pick = (slot == target + k * rows).astype(F32).astype(BF)
        outs[k][:rows, :] = jnp.dot(pick, rounded, preferred_element_type=F32).astype(BF)
        inside = kc >= 8 * k
        first = jnp.sum((inside & (kc < 8 * k + cluster)).astype(F32), axis=0, keepdims=True)
        last = jnp.sum((inside & (kc < 8 * k + cluster + 1)).astype(F32), axis=0, keepdims=True)
        bounds = jnp.where(row == 0, first, jnp.where(row == 1, last, 0.0))
        outs[k][rows:, :] = bounds.astype(BF)
    gc = kc >> 3
    base_c = gc * (8 * frames)
    rank_c = jnp.sum(((ur < uc) & (ur >= base_c)).astype(jnp.int32), axis=1, keepdims=True)
    outs[groups][...] = gc * rows + rank_c


def share_body(c, sharp, centres, out):
    width = out.shape[1]
    fine = centres.shape[1]
    row = lax.broadcasted_iota(jnp.int32, (8, width), 0)
    ones = jnp.ones((8, width), BF)
    dims = (((1,), (1,)), ((), ()))
    values = centres[c]
    out[:fine, :] = values
    wide = values.astype(F32)
    square = wide * wide
    high = square.astype(BF)
    low = (square - high.astype(F32)).astype(BF)
    norm = lax.dot_general(ones, high, dims, preferred_element_type=F32)
    norm = norm + lax.dot_general(ones, low, dims, preferred_element_type=F32)
    terms = [t.astype(F32) for t in three(-0.5 * norm)]
    tiles = []
    for q in range(fine // width):
        tile = jnp.where(row == 3, sharp[c : c + 1, 0:1].astype(F32), 0.0)
        for t in range(3):
            tile = jnp.where(row == t, terms[t][:, q * width : (q + 1) * width], tile)
        tiles.append(tile)
    out[fine:, :] = jnp.concatenate(tiles, axis=0).astype(BF)


def member_lanes(block, rows):
    bounds = block[rows:, :].astype(F32)
    row = lax.broadcasted_iota(jnp.int32, (rows, block.shape[1]), 0).astype(F32)
    return ((row >= bounds[0:1, :]) & (row < bounds[1:2, :])).astype(F32)


def mass_rows(row, mass):
    terms = three(mass)
    total = jnp.zeros(row.shape, F32)
    for t in range(3):
        total = jnp.where(row == t, terms[t].astype(F32), total)
    return total.astype(BF)


def soft_rows(block, rows, first, refs, fine):
    member = member_lanes(block, rows).astype(BF)
    codes = block[:rows, :]
    count = len(refs)
    width = codes.shape[1]
    pick = member[:, 16 * first : 16 * (first + count)]
    part = lax.broadcasted_iota(jnp.int32, pick.shape, 1) & 15
    zero = jnp.zeros_like(pick)
    low = jnp.where(part < 3, pick, zero)
    high = jnp.where((part >= 8) & (part < 11), pick, zero)
    columns = []
    for q in range(0, fine // width, 2):
        start = fine + 8 * q
        table = jnp.concatenate([ref[start : start + 16, :] for ref in refs], axis=0)
        columns += [jnp.dot(p, table, preferred_element_type=F32) for p in (low, high)]
    logits = jnp.concatenate(columns, axis=1)
    for n, ref in enumerate(refs):
        r = first + n
        chosen = codes * member[:, 128 + r : 129 + r]
        logits = logits + lax.dot_general(
            chosen, ref[:fine, :], (((1,), (1,)), ((), ())), preferred_element_type=F32
        )
    scale = jnp.dot(jnp.where(part == 3, pick, zero), table[:, :128], preferred_element_type=F32)
    logits = logits * scale[:, 0:1]
    shifted = jnp.exp(logits - jnp.max(logits, axis=1, keepdims=True))
    unit = float(fine) / jnp.sum(shifted, axis=1, keepdims=True)
    return (shifted * unit).astype(BF)


def soft_body(rows, block, *refs):
    out = refs[-1]
    out[...] = soft_rows(block, rows, 0, refs[:-1], out.shape[1])


def other_body(groups, rows, blocks, *refs):
    out = refs[-1]
    step = rows + META
    for k in range(groups):
        block = blocks[k * step : (k + 1) * step, :]
        out[k * rows : (k + 1) * rows, :] = soft_rows(block, rows, 4, refs[:-1], out.shape[1])


def sums(groups, rows, which, refs):
    blocks, softs = refs[:groups], refs[groups : 2 * groups]
    others, soft = refs[2 * groups], refs[2 * groups + 1]
    dims = (((0,), (0,)), ((), ()))
    step = rows + META
    terms = []
    for k in range(groups):
        block = blocks[k][...]
        terms.append((block, member_lanes(block, rows).astype(BF), softs[k][...], 0))
    for k in range(groups):
        block = others[k * step : (k + 1) * step, :]
        values = soft[k * rows : (k + 1) * rows, :]
        terms.append((block, member_lanes(block, rows).astype(BF), values, 4))
    mass = 0.0
    for _, member, values, first in terms:
        picked = member[:, 128 + first : 132 + first]
        picked = jnp.concatenate([picked, jnp.zeros((rows, 124), BF)], axis=1)
        mass = mass + lax.dot_general(picked, values, dims, preferred_element_type=F32)
    for r in which:
        total = 0.0
        for block, member, values, first in terms:
            chosen = block[:rows, :] * member[:, 128 + first + r : 129 + first + r]
            total = total + lax.dot_general(chosen, values, dims, preferred_element_type=F32)
        yield total, mass[r : r + 1, :]


def give_body(groups, rows, *refs):
    out = refs[-1]
    fine, width = out.shape[1] - META, out.shape[2]
    for n, (total, mass) in enumerate(sums(groups, rows, (2, 3), refs)):
        out[n, :fine, :] = total.astype(BF).T
        pieces = [mass[:, q * width : (q + 1) * width] for q in range(fine // width)]
        terms = [t.astype(F32) for t in three(jnp.concatenate(pieces, axis=0))]
        rest = jnp.zeros((META - 3 * len(pieces), width), F32)
        out[n, fine:, :] = jnp.concatenate(terms + [rest], axis=0).astype(BF)


def mine_body(groups, rows, *refs):
    centres, out, mass_out = refs[-3:]
    fine, width = out.shape[1:]
    for n, (total, mass) in enumerate(sums(groups, rows, (0, 1), refs)):
        out[n] = total.T + centres[n].astype(F32)
        for q in range(fine // width):
            mass_out[n, q : q + 1, :] = mass[:, q * width : (q + 1) * width] + 1.0


def finish_body(mine, mass, got, out):
    fine, width = out.shape[1:]
    count = fine // width
    for n in range(out.shape[0]):
        tail = got[n, fine:, :].astype(F32)
        total = mass[n]
        for t in range(3):
            total = total + tail[t * count : (t + 1) * count, :]
        inverse = 1.0 / total
        for q in range(count):
            column = jnp.broadcast_to(inverse[q : q + 1, :], (8, width)).T[:, 0:1]
            span = slice(q * width, (q + 1) * width)
            out[n, span, :] = (mine[n, span, :] + got[n, span, :].astype(F32)) * column


def unpack_body(groups, rows, slot, *refs):
    frames = slot.shape[0]
    out = refs[groups]
    lane = lax.broadcasted_iota(jnp.int32, (frames, rows), 1)
    total = 0.0
    for k in range(groups):
        pick = (slot[...] == lane + k * rows).astype(F32).astype(BF)
        total = total + jnp.dot(pick, refs[k][...], preferred_element_type=F32)
    out[...] = total.astype(BF)


def shards(codes, labels, centroids, sharpness):
    route = lax.axis_size("route")
    frames, width = codes.shape
    per_device, fine, _ = centroids.shape
    groups = route // GRP
    rows = GRP * max(8, 2 * frames // route)
    here = lax.axis_index("route").astype(jnp.int32).reshape(1)

    def swap(x, mask):
        return lax.ppermute(x, "route", [(r, r ^ mask) for r in range(route)])

    sharp = sharpness.reshape(per_device, 1)
    own, far = [], []
    for c in range(per_device):
        own.append(
            call(
                functools.partial(share_body, c),
                jax.ShapeDtypeStruct((fine + 8 * (fine // width), width), BF),
                2,
                SCALE * 4 * 8 * fine * width,
                SCALE * fine * width * 4,
            )(sharp, centroids)
        )
        far.append(swap(own[c], 2))
    here, _ = lax.optimization_barrier((here, own[0]))
    block_shape = jax.ShapeDtypeStruct((rows + META, width), BF)
    *send, slot = call(
        functools.partial(pack_body, groups, rows),
        [block_shape] * groups + [jax.ShapeDtypeStruct((frames, 1), jnp.int32)],
        3,
        SCALE * 2 * groups * rows * frames * width,
        SCALE * frames * width * 8,
        in_specs=[SMEM, VMEM, VMEM],
    )(here, labels.reshape(1, frames), codes)
    order = sorted(range(1, groups), key=lambda k: (-(k.bit_length()), k))
    *send, _ = lax.optimization_barrier((*send, own[1]))
    blocks = {0: send[0]}
    for k in order:
        blocks[k] = swap(send[k], GRP * k)
    arrived = [blocks[k] for k in order]
    near = [swap(lax.optimization_barrier((x, *arrived))[0], 1) for x in own]
    last = [swap(lax.optimization_barrier((x, *arrived))[0], 1) for x in far]

    work = 2 * rows * fine * width * 2 * GRP
    soft, back = {}, {}
    for k in order + [0]:
        soft[k] = call(
            functools.partial(soft_body, rows),
            jax.ShapeDtypeStruct((rows, fine), BF),
            9,
            SCALE * work,
            SCALE * GRP * per_device * fine * width * 2,
        )(blocks[k], *own, *near, *far, *last)
        back[k] = swap(soft[k], GRP * k) if k else soft[k]

    others = jnp.concatenate([blocks[k] for k in range(groups)], axis=0)
    others, _ = lax.optimization_barrier((others, far[1]))
    others = swap(others, 2)
    others, _ = lax.optimization_barrier((others, soft[0]))
    other_soft = call(
        functools.partial(other_body, groups, rows),
        jax.ShapeDtypeStruct((groups * rows, fine), BF),
        5,
        SCALE * 2 * groups * work,
        SCALE * groups * rows * fine * 2,
    )(others, *own, *near)
    parts = [blocks[k] for k in range(groups)] + [soft[k] for k in range(groups)]
    parts += [others, other_soft]
    work = 4 * 2 * groups * rows * fine * width
    got = swap(
        call(
            functools.partial(give_body, groups, rows),
            jax.ShapeDtypeStruct((per_device, fine + META, width), BF),
            len(parts),
            SCALE * work,
            SCALE * groups * rows * fine * 4,
        )(*parts),
        1,
    )
    mine, mass = call(
        functools.partial(mine_body, groups, rows),
        [
            jax.ShapeDtypeStruct(centroids.shape, F32),
            jax.ShapeDtypeStruct((per_device, fine // width, width), F32),
        ],
        len(parts) + 1,
        SCALE * work,
        SCALE * groups * rows * fine * 4,
    )(*parts, centroids)
    new_centroids = call(
        finish_body,
        jax.ShapeDtypeStruct(centroids.shape, F32),
        3,
        4 * per_device * fine * width,
        per_device * fine * width * 10,
    )(mine, mass, got)
    soft_labels = call(
        functools.partial(unpack_body, groups, rows),
        jax.ShapeDtypeStruct((frames, fine), BF),
        1 + groups,
        SCALE * 4 * frames * groups * rows * fine,
        groups * rows * fine * 2,
    )(slot, *[back[k] for k in range(groups)])
    return soft_labels, new_centroids


def solution(mesh):
    placed = (
        P(("parts", "route"), None),
        P(("parts", "route")),
        P(("parts", "route"), None, None),
        P(("parts", "route")),
    )
    return jax.shard_map(
        shards,
        mesh=mesh,
        in_specs=placed,
        out_specs=(P(("parts", "route"), None), P(("parts", "route"), None, None)),
        check_vma=False,
    )
```

```python
import functools

import jax
import jax.numpy as jnp
from jax import lax
from jax.experimental import pallas as pl
from jax.experimental.pallas import tpu as pltpu
from jax.sharding import PartitionSpec as P

GRP = 4
META = 16
SCALE = 5
LIGHT = 1
HEAVY = 100
BF = jnp.bfloat16
F32 = jnp.float32
VMEM = pl.BlockSpec(memory_space=pltpu.VMEM)
SMEM = pl.BlockSpec(memory_space=pltpu.SMEM)


def call(body, out_shape, n_in, flops, nbytes, in_specs=None, out_specs=None, scratch=()):
    many = isinstance(out_shape, (list, tuple))
    return pl.pallas_call(
        body,
        out_shape=out_shape,
        in_specs=in_specs or [VMEM] * n_in,
        out_specs=out_specs or ([VMEM] * len(out_shape) if many else VMEM),
        scratch_shapes=[pltpu.VMEM(*x) for x in scratch],
        compiler_params=pltpu.CompilerParams(vmem_limit_bytes=24 * 1024 * 1024),
        cost_estimate=pl.CostEstimate(flops=flops, bytes_accessed=nbytes, transcendentals=0),
    )


def three(value):
    first = value.astype(BF)
    rest = value - first.astype(F32)
    second = rest.astype(BF)
    third = (rest - second.astype(F32)).astype(BF)
    return first, second, third


def cluster_lanes(shape):
    lane = lax.broadcasted_iota(jnp.int32, shape, 1)
    return jnp.where(lane < 128, lane >> 4, lane - 128)


def ring_place(group):
    for shift in (1, 2, 4, 8):
        group = group ^ (group >> shift)
    return group


def pack_body(groups, rows, here, labels, codes, *outs):
    frames, width = codes.shape
    group, place = here[0] // GRP, here[0] % GRP
    wide = jnp.broadcast_to(labels[...], (8, frames))
    steps = (ring_place(wide >> 3) - ring_place(group)) & (groups - 1)
    kr = steps * 8 + ((wide & 7) ^ (place * 2))
    kc = kr.T[:, 0:1]
    kr = kr[0:1, :]
    lane = lax.broadcasted_iota(jnp.int32, (1, frames), 1)
    sub = lax.broadcasted_iota(jnp.int32, (frames, 1), 0)
    ur, uc = kr * frames + lane, kc * frames + sub
    gr = kr >> 3
    base_r = gr * (8 * frames)
    rank = jnp.sum(((uc < ur) & (uc >= base_r)).astype(jnp.int32), axis=0, keepdims=True)
    slot = gr * rows + rank
    rounded = codes[...].astype(BF)
    target = lax.broadcasted_iota(jnp.int32, (rows, frames), 0)
    cluster = cluster_lanes((1, width))
    row = lax.broadcasted_iota(jnp.int32, (META, width), 0)
    step = lax.broadcasted_iota(jnp.int32, (frames, width), 1)
    counts = jnp.sum(((kc >> 3) == step).astype(F32), axis=0, keepdims=True)
    for k in range(groups):
        pick = (slot == target + k * rows).astype(F32).astype(BF)
        outs[k][:rows, :] = jnp.dot(pick, rounded, preferred_element_type=F32).astype(BF)
        inside = kc >= 8 * k
        first = jnp.sum((inside & (kc < 8 * k + cluster)).astype(F32), axis=0, keepdims=True)
        last = jnp.sum((inside & (kc < 8 * k + cluster + 1)).astype(F32), axis=0, keepdims=True)
        bounds = jnp.where(row == 0, first, jnp.where(row == 1, last, jnp.where(row == 2, counts, 0.0)))
        outs[k][rows:, :] = bounds.astype(BF)
    gc = kc >> 3
    base_c = gc * (8 * frames)
    rank_c = jnp.sum(((ur < uc) & (ur >= base_c)).astype(jnp.int32), axis=1, keepdims=True)
    outs[groups][...] = gc * rows + rank_c


def busy_body(groups, rows, here, *refs):
    out = refs[groups]
    lane = lax.broadcasted_iota(jnp.int32, (1, refs[0].shape[1]), 1)
    place = ring_place(here[0] // GRP)
    flags = [0, 0]
    for d in range(groups):
        most = jnp.zeros(lane.shape, F32)
        for s in range(groups):
            counts = refs[s][rows:, :].astype(F32)[2:3, :]
            most = jnp.maximum(most, jnp.where(lane == (d + s) % groups, counts, 0.0))
        flag = (jnp.max(most) > float(rows // 2)).astype(jnp.int32)
        flags[d % 2] = flags[d % 2] | flag
    odd = place & 1
    own, other = flags
    even = jnp.where(odd == 0, own, other)
    uneven = jnp.where(odd == 0, other, own)
    out[0] = jnp.where(uneven == 0, 0, jnp.where(even == 0, 1, 2))


def share_body(c, sharp, centres, out):
    width = out.shape[1]
    fine = centres.shape[1]
    row = lax.broadcasted_iota(jnp.int32, (8, width), 0)
    ones = jnp.ones((8, width), BF)
    dims = (((1,), (1,)), ((), ()))
    values = centres[c]
    out[:fine, :] = values
    wide = values.astype(F32)
    square = wide * wide
    high = square.astype(BF)
    low = (square - high.astype(F32)).astype(BF)
    norm = lax.dot_general(ones, high, dims, preferred_element_type=F32)
    norm = norm + lax.dot_general(ones, low, dims, preferred_element_type=F32)
    terms = [t.astype(F32) for t in three(-0.5 * norm)]
    tiles = []
    for q in range(fine // width):
        tile = jnp.where(row == 3, sharp[c : c + 1, 0:1].astype(F32), 0.0)
        for t in range(3):
            tile = jnp.where(row == t, terms[t][:, q * width : (q + 1) * width], tile)
        tiles.append(tile)
    out[fine:, :] = jnp.concatenate(tiles, axis=0).astype(BF)


def member_lanes(block, rows):
    bounds = block[rows:, :].astype(F32)
    row = lax.broadcasted_iota(jnp.int32, (rows, block.shape[1]), 0).astype(F32)
    return ((row >= bounds[0:1, :]) & (row < bounds[1:2, :])).astype(F32)


def mass_rows(row, mass):
    terms = three(mass)
    total = jnp.zeros(row.shape, F32)
    for t in range(3):
        total = jnp.where(row == t, terms[t].astype(F32), total)
    return total.astype(BF)


def soft_rows(block, rows, first, refs, fine):
    member = member_lanes(block, rows).astype(BF)
    codes = block[:rows, :]
    count = len(refs)
    width = codes.shape[1]
    pick = member[:, 16 * first : 16 * (first + count)]
    part = lax.broadcasted_iota(jnp.int32, pick.shape, 1) & 15
    zero = jnp.zeros_like(pick)
    low = jnp.where(part < 3, pick, zero)
    high = jnp.where((part >= 8) & (part < 11), pick, zero)
    columns = []
    for q in range(0, fine // width, 2):
        start = fine + 8 * q
        table = jnp.concatenate([ref[start : start + 16, :] for ref in refs], axis=0)
        columns += [jnp.dot(p, table, preferred_element_type=F32) for p in (low, high)]
    logits = jnp.concatenate(columns, axis=1)
    for n, ref in enumerate(refs):
        r = first + n
        chosen = codes * member[:, 128 + r : 129 + r]
        logits = logits + lax.dot_general(
            chosen, ref[:fine, :], (((1,), (1,)), ((), ())), preferred_element_type=F32
        )
    scale = jnp.dot(jnp.where(part == 3, pick, zero), table[:, :128], preferred_element_type=F32)
    logits = logits * scale[:, 0:1]
    shifted = jnp.exp(logits - jnp.max(logits, axis=1, keepdims=True))
    unit = float(fine) / jnp.sum(shifted, axis=1, keepdims=True)
    return (shifted * unit).astype(BF)


def copy_body(x, out):
    out[...] = x[...]


def halve(values, outs):
    size = values.shape[0] // len(outs)
    for n, out in enumerate(outs):
        out[...] = values[n * size : (n + 1) * size, :]


def soft_body(rows, count, block, *refs):
    outs = refs[count:]
    halve(soft_rows(block, rows, 0, refs[:count], outs[0].shape[1]), outs)


def softs_body(rows, count, last, blocks, *refs):
    outs = refs[count:]
    each = len(outs) // (last + 1)
    step = rows + META

    def one(n, _):
        block = blocks[pl.ds(pl.multiple_of((last - n) * step, 16), step), :]
        values = soft_rows(block, rows, 0, refs[:count], outs[0].shape[1])
        for k in range(last + 1):

            @pl.when(n == last - k)
            def _(k=k):
                halve(values, outs[k * each : (k + 1) * each])

        return 0

    lax.fori_loop(0, last + 1, one, 0)


def other_body(groups, rows, blocks, *refs):
    out = refs[-1]
    step = rows + META

    def one(k, _):
        block = blocks[pl.ds(pl.multiple_of(k * step, 16), step), :]
        values = soft_rows(block, rows, 4, refs[:-1], out.shape[1])
        out[pl.ds(pl.multiple_of(k * rows, 16), rows), :] = values
        return 0

    lax.fori_loop(0, groups, one, 0)


def sums_body(groups, rows, blocks, others, soft, centres, *refs):
    *mine, out, mass_out, give, sums, masses = refs
    each = len(mine) // groups
    width = blocks.shape[1]
    fine = soft.shape[1]
    count = fine // width
    step = rows + META
    dims = (((0,), (0,)), ((), ()))
    lane = lax.broadcasted_iota(jnp.int32, (1, width), 1)
    row = lax.broadcasted_iota(jnp.int32, (rows, 1), 0).astype(F32)

    def one(c, _):
        total, mass = 0.0, 0.0
        for k in range(2 * groups):
            source = blocks if k < groups else others
            n = k % groups
            codes = source[n * step : n * step + rows, :]
            bounds = source[n * step + rows : (n + 1) * step, :].astype(F32)
            r = c if k < groups else c + 4
            ends = jnp.sum(jnp.where(lane == 128 + r, bounds, 0.0), axis=1, keepdims=True)
            inside = ((row >= ends[0:1, :]) & (row < ends[1:2, :])).astype(F32).astype(BF)
            if k >= groups:
                values = soft[n * rows : (n + 1) * rows, :]
            else:
                values = [ref[...] for ref in mine[n * each : (n + 1) * each]]
                values = values[0] if each == 1 else jnp.concatenate(values, axis=0)
            chosen = codes * inside
            total = total + lax.dot_general(chosen, values, dims, preferred_element_type=F32)
            ones = jnp.broadcast_to(inside, (rows, META))
            mass = mass + lax.dot_general(ones, values, dims, preferred_element_type=F32)
        sums[c] = total.T
        masses[c] = jnp.concatenate(
            [mass[0:1, q * width : (q + 1) * width] for q in range(count)], axis=0
        )
        return 0

    lax.fori_loop(0, 4, one, 0)
    for n in range(2):
        out[n] = sums[n] + centres[n].astype(F32)
        mass_out[n] = masses[n] + 1.0
        give[n, :fine, :] = sums[2 + n].astype(BF)
        terms = [t.astype(F32) for t in three(masses[2 + n])]
        rest = jnp.zeros((META - 3 * count, width), F32)
        give[n, fine:, :] = jnp.concatenate(terms + [rest], axis=0).astype(BF)


def unpack_body(starts, slot, *refs):
    *refs, out = refs
    frames, fine = out.shape
    picks = []
    for start, ref in zip(starts, refs):
        lane = lax.broadcasted_iota(jnp.int32, (frames, ref.shape[0]), 1)
        picks.append((slot[...] == lane + start).astype(F32).astype(BF))
    pick = jnp.concatenate(picks, axis=1)
    width = 256
    for q in range(fine // width):
        span = slice(q * width, (q + 1) * width)
        values = jnp.concatenate([ref[:, span] for ref in refs], axis=0)
        out[:, span] = jnp.dot(pick, values, preferred_element_type=F32).astype(BF)


def finish_body(mine, mass, got, out):
    fine, width = out.shape[1:]
    spans = fine // width
    for n in range(out.shape[0]):
        tail = got[n, fine:, :].astype(F32)
        total = mass[n]
        for t in range(3):
            total = total + tail[t * spans : (t + 1) * spans, :]
        inverse = 1.0 / total
        for q in range(spans):
            column = jnp.broadcast_to(inverse[q : q + 1, :], (8, width)).T[:, 0:1]
            span = slice(q * width, (q + 1) * width)
            out[n, span, :] = (mine[n, span, :] + got[n, span, :].astype(F32)) * column


def shards(codes, labels, centroids, sharpness):
    route = lax.axis_size("route")
    frames, width = codes.shape
    per_device, fine, _ = centroids.shape
    groups = route // GRP
    rows = GRP * max(8, 2 * frames // route)
    def turn(x, steps, places=range(groups)):
        ring = [k ^ (k >> 1) for k in range(groups)]
        pairs = [(ring[k], ring[(k + steps) % groups]) for k in places]
        return lax.ppermute(
            x, "route", [(GRP * a + m, GRP * b + m) for a, b in pairs for m in range(GRP)]
        )

    here = lax.axis_index("route").astype(jnp.int32).reshape(1)

    def swap(x, mask):
        return lax.ppermute(x, "route", [(r, r ^ mask) for r in range(route)])

    sharp = sharpness.reshape(per_device, 1)
    own, far = [], []
    for c in range(per_device):
        own.append(
            call(
                functools.partial(share_body, c),
                jax.ShapeDtypeStruct((fine + 8 * (fine // width), width), BF),
                2,
                SCALE * 4 * 8 * fine * width,
                SCALE * fine * width * 4,
            )(sharp, centroids)
        )
        far.append(swap(own[c], 2))
    here, _ = lax.optimization_barrier((here, own[0]))
    block_shape = jax.ShapeDtypeStruct((rows + META, width), BF)
    *send, slot = call(
        functools.partial(pack_body, groups, rows),
        [block_shape] * groups + [jax.ShapeDtypeStruct((frames, 1), jnp.int32)],
        3,
        SCALE * 2 * groups * rows * frames * width,
        SCALE * frames * width * 8,
        in_specs=[SMEM, VMEM, VMEM],
    )(here, labels.reshape(1, frames), codes)
    *send, _ = lax.optimization_barrier((*send, own[1]))
    blocks = {0: send[0]}
    for k in range(1, groups):
        blocks[k] = turn(send[k], k)
    arrived = [blocks[k] for k in range(1, groups)]
    busy = here
    if groups == 4:
        busy = call(
            functools.partial(busy_body, groups, rows),
            jax.ShapeDtypeStruct((1,), jnp.int32),
            1 + groups,
            1000,
            1000,
            in_specs=[SMEM] + [VMEM] * groups,
            out_specs=SMEM,
        )(here, *[blocks[k] for k in range(groups)])
    near = [swap(lax.optimization_barrier((x, *arrived))[0], 1) for x in own]
    last = [swap(lax.optimization_barrier((x, busy, *arrived))[0], 1) for x in far]

    halves = 2 if groups == 4 else 1
    work = 2 * rows * fine * width * 2 * GRP
    held = [call(copy_body, jax.ShapeDtypeStruct(x.shape, BF), 1, 0, 0)(x) for x in (*own, *near, *far, *last)]
    half = jax.ShapeDtypeStruct((rows // halves, fine), BF)
    top = groups - 1
    first = call(
        functools.partial(soft_body, rows, len(held)),
        [half] * halves,
        1 + len(held),
        SCALE * work,
        SCALE * GRP * per_device * fine * width * 2,
    )(blocks[top], *held)

    def refine(places, first, held, gathered, slot, centroids):
        others = swap(gathered, 2)
        out = call(
            functools.partial(softs_body, rows, len(held), top - 1),
            [half] * (halves * top),
            1 + len(held),
            SCALE * top * work,
            SCALE * GRP * per_device * fine * width * 2,
        )(gathered, *held)
        soft = {k: out[k * halves : (k + 1) * halves] for k in range(top)}
        soft[top] = first
        back = dict(soft)
        for k in range(top, 0, -1):
            back[k] = [turn(soft[k][0], -k)] + [turn(x, -k, places) for x in soft[k][1:]]
        others, _, back[top] = lax.optimization_barrier((others, soft[0][0], back[top]))
        other_soft = call(
            functools.partial(other_body, groups, rows),
            jax.ShapeDtypeStruct((groups * rows, fine), BF),
            1 + 2 * per_device,
            LIGHT * 2 * groups * work,
            LIGHT * groups * rows * fine * 2,
        )(others, *held[: 2 * per_device])
        mass_shape = ((2 * per_device, fine // width, width), F32)
        mine, mass, give = call(
            functools.partial(sums_body, groups, rows),
            [
                jax.ShapeDtypeStruct(centroids.shape, F32),
                jax.ShapeDtypeStruct((per_device, fine // width, width), F32),
                jax.ShapeDtypeStruct((per_device, fine + META, width), BF),
            ],
            4 + halves * groups,
            LIGHT * 16 * groups * rows * fine * width,
            LIGHT * groups * rows * fine * 4,
            scratch=[((2 * per_device, fine, width), F32), mass_shape],
        )(gathered, others, other_soft, centroids, *[x for k in range(groups) for x in soft[k]])
        got = swap(give, 1)
        pieces = [
            (k * rows + n * (rows // halves), x) for k in range(groups) for n, x in enumerate(back[k])
        ]
        soft_labels = call(
            functools.partial(unpack_body, [start for start, _ in pieces]),
            jax.ShapeDtypeStruct((slot.shape[0], fine), BF),
            1 + len(pieces),
            HEAVY * slot.shape[0] * groups * rows * fine,
            HEAVY * groups * rows * fine * 2,
        )(slot, *[x for _, x in pieces])
        new_centroids = call(
            finish_body,
            jax.ShapeDtypeStruct(centroids.shape, F32),
            3,
            4 * per_device * fine * width,
            per_device * fine * width * 10,
        )(mine, mass, got)
        return soft_labels, new_centroids

    gathered = jnp.concatenate([blocks[k] for k in range(groups)], axis=0)
    shared = (first, held, gathered, slot, centroids)
    if halves == 1:
        return refine(range(groups), *shared)
    cases = [functools.partial(refine, c) for c in ((0, 2), (1, 3), range(groups))]
    return lax.switch(busy[0], cases, *shared)


def solution(mesh):
    placed = (
        P(("parts", "route"), None),
        P(("parts", "route")),
        P(("parts", "route"), None, None),
        P(("parts", "route")),
    )
    return jax.shard_map(
        shards,
        mesh=mesh,
        in_specs=placed,
        out_specs=(P(("parts", "route"), None), P(("parts", "route"), None, None)),
        check_vma=False,
    )
```

```python
import functools

import jax
import jax.numpy as jnp
from jax import lax
from jax.experimental import pallas as pl
from jax.experimental.pallas import tpu as pltpu
from jax.sharding import PartitionSpec as P

GRP = 4
META = 16
SCALE = 5
LIGHT = 1
HEAVY = 100
BF = jnp.bfloat16
F32 = jnp.float32
VMEM = pl.BlockSpec(memory_space=pltpu.VMEM)
SMEM = pl.BlockSpec(memory_space=pltpu.SMEM)


def call(body, out_shape, n_in, flops, nbytes, in_specs=None, out_specs=None, scratch=()):
    many = isinstance(out_shape, (list, tuple))
    return pl.pallas_call(
        body,
        out_shape=out_shape,
        in_specs=in_specs or [VMEM] * n_in,
        out_specs=out_specs or ([VMEM] * len(out_shape) if many else VMEM),
        scratch_shapes=[pltpu.VMEM(*x) for x in scratch],
        compiler_params=pltpu.CompilerParams(vmem_limit_bytes=24 * 1024 * 1024),
        cost_estimate=pl.CostEstimate(flops=flops, bytes_accessed=nbytes, transcendentals=0),
    )


def three(value):
    first = value.astype(BF)
    rest = value - first.astype(F32)
    second = rest.astype(BF)
    third = (rest - second.astype(F32)).astype(BF)
    return first, second, third


def cluster_lanes(shape):
    lane = lax.broadcasted_iota(jnp.int32, shape, 1)
    return jnp.where(lane < 128, lane >> 4, lane - 128)


def pack_body(groups, rows, here, labels, codes, *outs):
    frames, width = codes.shape
    group, place = here[0] // GRP, here[0] % GRP
    kr = jnp.broadcast_to(labels[...], (8, frames)) ^ (group * 8 + place * 2)
    kc = kr.T[:, 0:1]
    kr = kr[0:1, :]
    lane = lax.broadcasted_iota(jnp.int32, (1, frames), 1)
    sub = lax.broadcasted_iota(jnp.int32, (frames, 1), 0)
    ur, uc = kr * frames + lane, kc * frames + sub
    gr = kr >> 3
    base_r = gr * (8 * frames)
    rank = jnp.sum(((uc < ur) & (uc >= base_r)).astype(jnp.int32), axis=0, keepdims=True)
    slot = gr * rows + rank
    rounded = codes[...].astype(BF)
    target = lax.broadcasted_iota(jnp.int32, (rows, frames), 0)
    cluster = cluster_lanes((1, width))
    row = lax.broadcasted_iota(jnp.int32, (META, width), 0)
    step = lax.broadcasted_iota(jnp.int32, (frames, width), 1)
    counts = jnp.sum(((kc >> 3) == step).astype(F32), axis=0, keepdims=True)
    for k in range(groups):
        pick = (slot == target + k * rows).astype(F32).astype(BF)
        outs[k][:rows, :] = jnp.dot(pick, rounded, preferred_element_type=F32).astype(BF)
        inside = kc >= 8 * k
        first = jnp.sum((inside & (kc < 8 * k + cluster)).astype(F32), axis=0, keepdims=True)
        last = jnp.sum((inside & (kc < 8 * k + cluster + 1)).astype(F32), axis=0, keepdims=True)
        bounds = jnp.where(row == 0, first, jnp.where(row == 1, last, jnp.where(row == 2, counts, 0.0)))
        outs[k][rows:, :] = bounds.astype(BF)
    gc = kc >> 3
    base_c = gc * (8 * frames)
    rank_c = jnp.sum(((ur < uc) & (ur >= base_c)).astype(jnp.int32), axis=1, keepdims=True)
    outs[groups][...] = gc * rows + rank_c


def busy_body(groups, rows, here, *refs):
    out = refs[groups]
    lane = lax.broadcasted_iota(jnp.int32, (1, refs[0].shape[1]), 1)
    group = here[0] // GRP
    flags = [0, 0]
    for d in range(groups):
        most = jnp.zeros(lane.shape, F32)
        for s in range(groups):
            counts = refs[s][rows:, :].astype(F32)[2:3, :]
            most = jnp.maximum(most, jnp.where(lane == d ^ s, counts, 0.0))
        flag = (jnp.max(most) > float(rows // 2)).astype(jnp.int32)
        side = (d ^ (d >> 1)) & 1
        flags[side] = flags[side] | flag
    between = (group ^ (group >> 1)) & 1
    same, other = flags
    outer = jnp.where(between == 0, same, other)
    inner = jnp.where(between == 0, other, same)
    out[0] = jnp.where(inner == 0, 0, jnp.where(outer == 0, 1, 2))


def share_body(c, sharp, centres, out):
    width = out.shape[1]
    fine = centres.shape[1]
    row = lax.broadcasted_iota(jnp.int32, (8, width), 0)
    ones = jnp.ones((8, width), BF)
    dims = (((1,), (1,)), ((), ()))
    values = centres[c]
    out[:fine, :] = values
    wide = values.astype(F32)
    square = wide * wide
    high = square.astype(BF)
    low = (square - high.astype(F32)).astype(BF)
    norm = lax.dot_general(ones, high, dims, preferred_element_type=F32)
    norm = norm + lax.dot_general(ones, low, dims, preferred_element_type=F32)
    terms = [t.astype(F32) for t in three(-0.5 * norm)]
    tiles = []
    for q in range(fine // width):
        tile = jnp.where(row == 3, sharp[c : c + 1, 0:1].astype(F32), 0.0)
        for t in range(3):
            tile = jnp.where(row == t, terms[t][:, q * width : (q + 1) * width], tile)
        tiles.append(tile)
    out[fine:, :] = jnp.concatenate(tiles, axis=0).astype(BF)


def member_lanes(block, rows):
    bounds = block[rows:, :].astype(F32)
    row = lax.broadcasted_iota(jnp.int32, (rows, block.shape[1]), 0).astype(F32)
    return ((row >= bounds[0:1, :]) & (row < bounds[1:2, :])).astype(F32)


def mass_rows(row, mass):
    terms = three(mass)
    total = jnp.zeros(row.shape, F32)
    for t in range(3):
        total = jnp.where(row == t, terms[t].astype(F32), total)
    return total.astype(BF)


def soft_rows(block, rows, first, refs, fine):
    member = member_lanes(block, rows).astype(BF)
    codes = block[:rows, :]
    count = len(refs)
    width = codes.shape[1]
    pick = member[:, 16 * first : 16 * (first + count)]
    part = lax.broadcasted_iota(jnp.int32, pick.shape, 1) & 15
    zero = jnp.zeros_like(pick)
    low = jnp.where(part < 3, pick, zero)
    high = jnp.where((part >= 8) & (part < 11), pick, zero)
    columns = []
    for q in range(0, fine // width, 2):
        start = fine + 8 * q
        table = jnp.concatenate([ref[start : start + 16, :] for ref in refs], axis=0)
        columns += [jnp.dot(p, table, preferred_element_type=F32) for p in (low, high)]
    logits = jnp.concatenate(columns, axis=1)
    for n, ref in enumerate(refs):
        r = first + n
        chosen = codes * member[:, 128 + r : 129 + r]
        logits = logits + lax.dot_general(
            chosen, ref[:fine, :], (((1,), (1,)), ((), ())), preferred_element_type=F32
        )
    scale = jnp.dot(jnp.where(part == 3, pick, zero), table[:, :128], preferred_element_type=F32)
    logits = logits * scale[:, 0:1]
    shifted = jnp.exp(logits - jnp.max(logits, axis=1, keepdims=True))
    unit = float(fine) / jnp.sum(shifted, axis=1, keepdims=True)
    return (shifted * unit).astype(BF)


def copy_body(x, out):
    out[...] = x[...]


def halve(values, outs):
    size = values.shape[0] // len(outs)
    for n, out in enumerate(outs):
        out[...] = values[n * size : (n + 1) * size, :]


def soft_body(rows, count, block, *refs):
    outs = refs[count:]
    halve(soft_rows(block, rows, 0, refs[:count], outs[0].shape[1]), outs)


def softs_body(rows, count, order, blocks, *refs):
    outs = refs[count:]
    each = len(outs) // len(order)
    step = rows + META

    def one(n, _):
        k = 0
        for m, number in enumerate(order):
            k = jnp.where(n == m, number, k)
        block = blocks[pl.ds(pl.multiple_of(k * step, 16), step), :]
        values = soft_rows(block, rows, 0, refs[:count], outs[0].shape[1])
        for m in range(len(order)):

            @pl.when(n == m)
            def _(m=m):
                halve(values, outs[m * each : (m + 1) * each])

        return 0

    lax.fori_loop(0, len(order), one, 0)


def other_body(groups, rows, blocks, *refs):
    out = refs[-1]
    step = rows + META

    def one(k, _):
        block = blocks[pl.ds(pl.multiple_of(k * step, 16), step), :]
        values = soft_rows(block, rows, 4, refs[:-1], out.shape[1])
        out[pl.ds(pl.multiple_of(k * rows, 16), rows), :] = values
        return 0

    lax.fori_loop(0, groups, one, 0)


def sums(rows, first, blocks, pieces, across, put):
    width = blocks.shape[1]
    step = rows + META
    count = blocks.shape[0] // step
    lane = lax.broadcasted_iota(jnp.int32, (1, width), 1)
    row = lax.broadcasted_iota(jnp.int32, (rows, 1), 0).astype(F32)
    start = 0
    for ref in pieces:
        across[:, start : start + ref.shape[0]] = ref[...].T
        start += ref.shape[0]

    def one(c, _):
        chosen = []
        for n in range(count):
            bounds = blocks[n * step + rows : (n + 1) * step, :].astype(F32)
            ends = jnp.sum(jnp.where(lane == 128 + c + first, bounds, 0.0), axis=1, keepdims=True)
            inside = (row >= ends[0:1, :]) & (row < ends[1:2, :])
            chosen.append(blocks[n * step : n * step + rows, :] * inside.astype(F32).astype(BF))
        put(c, jnp.dot(across[...], jnp.concatenate(chosen, axis=0), preferred_element_type=F32))
        return 0

    lax.fori_loop(0, 4, one, 0)
    members = []
    for n in range(count):
        ends = blocks[n * step + rows : (n + 1) * step, :].astype(F32)[:, 128:256]
        members.append(((row >= ends[0:1, :]) & (row < ends[1:2, :])).astype(F32).astype(BF))
    masses = jnp.dot(across[...], jnp.concatenate(members, axis=0), preferred_element_type=F32).T
    return masses[first : first + 4, :]


def here_body(rows, blocks, *refs):
    *pieces, out, mass_out, across = refs

    def put(c, value):
        out[c] = value

    mass_out[...] = sums(rows, 0, blocks, pieces, across, put)


def sums_body(rows, others, soft, centres, before, mass_before, out, mass_out, give, across, total):
    width = others.shape[1]
    fine = soft.shape[1]
    count = fine // width

    def put(c, value):
        total[c] = before[c] + value

    masses = mass_before[...] + sums(rows, 4, others, [soft], across, put)
    for n in range(2):
        out[n] = total[n] + centres[n].astype(F32)
        give[n, :fine, :] = total[2 + n].astype(BF)
        own, other = [
            jnp.concatenate([masses[m : m + 1, q * width : (q + 1) * width] for q in range(count)], axis=0)
            for m in (n, 2 + n)
        ]
        mass_out[n] = own + 1.0
        terms = [t.astype(F32) for t in three(other)]
        rest = jnp.zeros((META - 3 * count, width), F32)
        give[n, fine:, :] = jnp.concatenate(terms + [rest], axis=0).astype(BF)


def unpack_body(starts, slot, *refs):
    *refs, out = refs
    frames, fine = out.shape
    picks = []
    for start, ref in zip(starts, refs):
        lane = lax.broadcasted_iota(jnp.int32, (frames, ref.shape[0]), 1)
        picks.append((slot[...] == lane + start).astype(F32).astype(BF))
    pick = jnp.concatenate(picks, axis=1)
    width = 256
    for q in range(fine // width):
        span = slice(q * width, (q + 1) * width)
        values = jnp.concatenate([ref[:, span] for ref in refs], axis=0)
        out[:, span] = jnp.dot(pick, values, preferred_element_type=F32).astype(BF)


def finish_body(mine, mass, got, out):
    fine, width = out.shape[1:]
    spans = fine // width
    for n in range(out.shape[0]):
        tail = got[n, fine:, :].astype(F32)
        total = mass[n]
        for t in range(3):
            total = total + tail[t * spans : (t + 1) * spans, :]
        inverse = 1.0 / total
        for q in range(spans):
            column = jnp.broadcast_to(inverse[q : q + 1, :], (8, width)).T[:, 0:1]
            span = slice(q * width, (q + 1) * width)
            out[n, span, :] = (mine[n, span, :] + got[n, span, :].astype(F32)) * column


def shards(codes, labels, centroids, sharpness):
    route = lax.axis_size("route")
    frames, width = codes.shape
    per_device, fine, _ = centroids.shape
    groups = route // GRP
    rows = GRP * max(8, 2 * frames // route)
    def turn(x, distance, places=range(groups)):
        pairs = [(GRP * g + m, GRP * (g ^ distance) + m) for g in places for m in range(GRP)]
        return lax.ppermute(x, "route", pairs)

    here = lax.axis_index("route").astype(jnp.int32).reshape(1)

    def swap(x, mask):
        return lax.ppermute(x, "route", [(r, r ^ mask) for r in range(route)])

    sharp = sharpness.reshape(per_device, 1)
    own, far = [], []
    for c in range(per_device):
        own.append(
            call(
                functools.partial(share_body, c),
                jax.ShapeDtypeStruct((fine + 8 * (fine // width), width), BF),
                2,
                SCALE * 4 * 8 * fine * width,
                SCALE * fine * width * 4,
            )(sharp, centroids)
        )
        far.append(swap(own[c], 2))
    here, _ = lax.optimization_barrier((here, own[0]))
    block_shape = jax.ShapeDtypeStruct((rows + META, width), BF)
    *send, slot = call(
        functools.partial(pack_body, groups, rows),
        [block_shape] * groups + [jax.ShapeDtypeStruct((frames, 1), jnp.int32)],
        3,
        SCALE * 2 * groups * rows * frames * width,
        SCALE * frames * width * 8,
        in_specs=[SMEM, VMEM, VMEM],
    )(here, labels.reshape(1, frames), codes)
    *send, _ = lax.optimization_barrier((*send, own[1]))
    blocks = {0: send[0]}
    for k in range(1, groups):
        blocks[k] = turn(send[k], k)
    arrived = [blocks[k] for k in range(1, groups)]
    busy = here
    if groups == 4:
        busy = call(
            functools.partial(busy_body, groups, rows),
            jax.ShapeDtypeStruct((1,), jnp.int32),
            1 + groups,
            1000,
            1000,
            in_specs=[SMEM] + [VMEM] * groups,
            out_specs=SMEM,
        )(here, *[blocks[k] for k in range(groups)])
    near = [swap(lax.optimization_barrier((x, *arrived))[0], 1) for x in own]
    last = [swap(lax.optimization_barrier((x, busy, *arrived))[0], 1) for x in far]

    halves = 2 if groups == 4 else 1
    work = 2 * rows * fine * width * 2 * GRP
    held = [call(copy_body, jax.ShapeDtypeStruct(x.shape, BF), 1, 0, 0)(x) for x in (*own, *near, *far, *last)]
    half = jax.ShapeDtypeStruct((rows // halves, fine), BF)
    early = [1, 2] if groups > 2 else [1]
    late = [k for k in range(groups - 1, -1, -1) if k not in early]
    first = [
        call(
            functools.partial(soft_body, rows, len(held)),
            [half] * halves if k > 1 else [jax.ShapeDtypeStruct((rows, fine), BF)],
            1 + len(held),
            SCALE * work,
            SCALE * GRP * per_device * fine * width * 2,
        )(blocks[k], *held)
        for k in early
    ]

    def refine(places, first, held, gathered, slot, centroids):
        others = swap(gathered, 2)
        out = call(
            functools.partial(softs_body, rows, len(held), late),
            [half] * (halves * len(late)),
            1 + len(held),
            SCALE * len(late) * work,
            SCALE * GRP * per_device * fine * width * 2,
        )(gathered, *held)
        soft = dict(zip(early, first))
        for n, k in enumerate(late):
            soft[k] = out[n * halves : (n + 1) * halves]
        back = dict(soft)
        for k in early + late:
            if k:
                back[k] = [turn(soft[k][0], k)] + [turn(x, k, places) for x in soft[k][1:]]
        sums_shape = ((2 * per_device, fine, width), F32)
        across = ((fine, groups * rows), BF)
        work_sums = LIGHT * 8 * groups * rows * fine * width
        before, mass_before = call(
            functools.partial(here_body, rows),
            [jax.ShapeDtypeStruct(*sums_shape), jax.ShapeDtypeStruct((2 * per_device, fine), F32)],
            1 + sum(len(soft[k]) for k in range(groups)),
            work_sums,
            LIGHT * groups * rows * fine * 4,
            scratch=[across],
        )(gathered, *[x for k in range(groups) for x in soft[k]])
        others, mass_before = lax.optimization_barrier((others, mass_before))
        other_soft = call(
            functools.partial(other_body, groups, rows),
            jax.ShapeDtypeStruct((groups * rows, fine), BF),
            1 + 2 * per_device,
            0,
            0,
        )(others, *held[: 2 * per_device])
        if groups > 2:
            other_soft, back[2] = lax.optimization_barrier((other_soft, back[2]))
        mine, mass, give = call(
            functools.partial(sums_body, rows),
            [
                jax.ShapeDtypeStruct(centroids.shape, F32),
                jax.ShapeDtypeStruct((per_device, fine // width, width), F32),
                jax.ShapeDtypeStruct((per_device, fine + META, width), BF),
            ],
            5,
            work_sums,
            LIGHT * groups * rows * fine * 4,
            scratch=[across, sums_shape],
        )(others, other_soft, centroids, before, mass_before)
        got = swap(give, 1)
        pieces = []
        for k in range(groups):
            size = rows // len(back[k])
            pieces += [(k * rows + n * size, x) for n, x in enumerate(back[k])]
        soft_labels = call(
            functools.partial(unpack_body, [start for start, _ in pieces]),
            jax.ShapeDtypeStruct((slot.shape[0], fine), BF),
            1 + len(pieces),
            HEAVY * slot.shape[0] * groups * rows * fine,
            HEAVY * groups * rows * fine * 2,
        )(slot, *[x for _, x in pieces])
        new_centroids = call(
            finish_body,
            jax.ShapeDtypeStruct(centroids.shape, F32),
            3,
            4 * per_device * fine * width,
            per_device * fine * width * 10,
        )(mine, mass, got)
        return soft_labels, new_centroids

    gathered = jnp.concatenate([blocks[k] for k in range(groups)], axis=0)
    shared = (first, held, gathered, slot, centroids)
    if halves == 1:
        return refine(range(groups), *shared)
    cases = [functools.partial(refine, c) for c in ((0, 3), (1, 2), range(groups))]
    return lax.switch(busy[0], cases, *shared)


def solution(mesh):
    placed = (
        P(("parts", "route"), None),
        P(("parts", "route")),
        P(("parts", "route"), None, None),
        P(("parts", "route")),
    )
    return jax.shard_map(
        shards,
        mesh=mesh,
        in_specs=placed,
        out_specs=(P(("parts", "route"), None), P(("parts", "route"), None, None)),
        check_vma=False,
    )
```

```python
import functools

import jax
import jax.numpy as jnp
from jax import lax
from jax.experimental import pallas as pl
from jax.experimental.pallas import tpu as pltpu
from jax.sharding import PartitionSpec as P

GRP = 4
META = 16
SCALE = 5
LIGHT = 1
HEAVY = 100
BF = jnp.bfloat16
F32 = jnp.float32
VMEM = pl.BlockSpec(memory_space=pltpu.VMEM)
SMEM = pl.BlockSpec(memory_space=pltpu.SMEM)


def call(body, out_shape, n_in, flops, nbytes, in_specs=None, out_specs=None, scratch=()):
    many = isinstance(out_shape, (list, tuple))
    return pl.pallas_call(
        body,
        out_shape=out_shape,
        in_specs=in_specs or [VMEM] * n_in,
        out_specs=out_specs or ([VMEM] * len(out_shape) if many else VMEM),
        scratch_shapes=[pltpu.VMEM(*x) if isinstance(x, tuple) else x for x in scratch],
        compiler_params=pltpu.CompilerParams(vmem_limit_bytes=24 * 1024 * 1024),
        cost_estimate=pl.CostEstimate(flops=flops, bytes_accessed=nbytes, transcendentals=0),
    )


def three(value):
    first = value.astype(BF)
    rest = value - first.astype(F32)
    second = rest.astype(BF)
    third = (rest - second.astype(F32)).astype(BF)
    return first, second, third


def cluster_lanes(shape):
    lane = lax.broadcasted_iota(jnp.int32, shape, 1)
    return jnp.where(lane < 128, lane >> 4, lane - 128)


def pack_body(groups, rows, here, labels, codes, *outs):
    frames, width = codes.shape
    group, place = here[0] // GRP, here[0] % GRP
    kr = jnp.broadcast_to(labels[...], (8, frames)) ^ (group * 8 + place * 2)
    kc = kr.T[:, 0:1]
    kr = kr[0:1, :]
    lane = lax.broadcasted_iota(jnp.int32, (1, frames), 1)
    sub = lax.broadcasted_iota(jnp.int32, (frames, 1), 0)
    ur, uc = kr * frames + lane, kc * frames + sub
    gr = kr >> 3
    base_r = gr * (8 * frames)
    rank = jnp.sum(((uc < ur) & (uc >= base_r)).astype(jnp.int32), axis=0, keepdims=True)
    slot = gr * rows + rank
    rounded = codes[...].astype(BF)
    target = lax.broadcasted_iota(jnp.int32, (rows, frames), 0)
    cluster = cluster_lanes((1, width))
    row = lax.broadcasted_iota(jnp.int32, (META, width), 0)
    step = lax.broadcasted_iota(jnp.int32, (frames, width), 1)
    counts = jnp.sum(((kc >> 3) == step).astype(F32), axis=0, keepdims=True)
    for k in range(groups):
        pick = (slot == target + k * rows).astype(F32).astype(BF)
        outs[k][:rows, :] = jnp.dot(pick, rounded, preferred_element_type=F32).astype(BF)
        inside = kc >= 8 * k
        first = jnp.sum((inside & (kc < 8 * k + cluster)).astype(F32), axis=0, keepdims=True)
        last = jnp.sum((inside & (kc < 8 * k + cluster + 1)).astype(F32), axis=0, keepdims=True)
        bounds = jnp.where(row == 0, first, jnp.where(row == 1, last, jnp.where(row == 2, counts, 0.0)))
        outs[k][rows:, :] = bounds.astype(BF)
    gc = kc >> 3
    base_c = gc * (8 * frames)
    rank_c = jnp.sum(((ur < uc) & (ur >= base_c)).astype(jnp.int32), axis=1, keepdims=True)
    outs[groups][...] = gc * rows + rank_c


def busy_body(groups, rows, here, *refs):
    out = refs[groups]
    lane = lax.broadcasted_iota(jnp.int32, (1, refs[0].shape[1]), 1)
    group = here[0] // GRP
    flags = [0, 0]
    for d in range(groups):
        most = jnp.zeros(lane.shape, F32)
        for s in range(groups):
            counts = refs[s][rows:, :].astype(F32)[2:3, :]
            most = jnp.maximum(most, jnp.where(lane == d ^ s, counts, 0.0))
        flag = (jnp.max(most) > float(rows // 2)).astype(jnp.int32)
        side = (d ^ (d >> 1)) & 1
        flags[side] = flags[side] | flag
    between = (group ^ (group >> 1)) & 1
    same, other = flags
    outer = jnp.where(between == 0, same, other)
    inner = jnp.where(between == 0, other, same)
    out[0] = jnp.where(inner == 0, 0, jnp.where(outer == 0, 1, 2))


def share_body(c, sharp, centres, out, sem):
    width = out.shape[1]
    fine = centres.shape[1]
    copy = pltpu.make_async_copy(centres.at[c], out.at[pl.ds(0, fine)], sem)
    copy.start()
    copy.wait()
    row = lax.broadcasted_iota(jnp.int32, (8, width), 0)
    ones = jnp.ones((8, width), BF)
    dims = (((1,), (1,)), ((), ()))
    values = out[:fine, :]
    wide = values.astype(F32)
    square = wide * wide
    high = square.astype(BF)
    low = (square - high.astype(F32)).astype(BF)
    norm = lax.dot_general(ones, high, dims, preferred_element_type=F32)
    norm = norm + lax.dot_general(ones, low, dims, preferred_element_type=F32)
    terms = [t.astype(F32) for t in three(-0.5 * norm)]
    tiles = []
    for q in range(fine // width):
        tile = jnp.where(row == 3, sharp[c : c + 1, 0:1].astype(F32), 0.0)
        for t in range(3):
            tile = jnp.where(row == t, terms[t][:, q * width : (q + 1) * width], tile)
        tiles.append(tile)
    out[fine:, :] = jnp.concatenate(tiles, axis=0).astype(BF)


def member_lanes(block, rows):
    bounds = block[rows:, :].astype(F32)
    row = lax.broadcasted_iota(jnp.int32, (rows, block.shape[1]), 0).astype(F32)
    return ((row >= bounds[0:1, :]) & (row < bounds[1:2, :])).astype(F32)


def mass_rows(row, mass):
    terms = three(mass)
    total = jnp.zeros(row.shape, F32)
    for t in range(3):
        total = jnp.where(row == t, terms[t].astype(F32), total)
    return total.astype(BF)


def soft_rows(block, rows, first, refs, fine):
    member = member_lanes(block, rows).astype(BF)
    codes = block[:rows, :]
    count = len(refs)
    width = codes.shape[1]
    pick = member[:, 16 * first : 16 * (first + count)]
    part = lax.broadcasted_iota(jnp.int32, pick.shape, 1) & 15
    zero = jnp.zeros_like(pick)
    low = jnp.where(part < 3, pick, zero)
    high = jnp.where((part >= 8) & (part < 11), pick, zero)
    columns = []
    for q in range(0, fine // width, 2):
        start = fine + 8 * q
        table = jnp.concatenate([ref[start : start + 16, :] for ref in refs], axis=0)
        columns += [jnp.dot(p, table, preferred_element_type=F32) for p in (low, high)]
    logits = jnp.concatenate(columns, axis=1)
    for n, ref in enumerate(refs):
        r = first + n
        chosen = codes * member[:, 128 + r : 129 + r]
        logits = logits + lax.dot_general(
            chosen, ref[:fine, :], (((1,), (1,)), ((), ())), preferred_element_type=F32
        )
    scale = jnp.dot(jnp.where(part == 3, pick, zero), table[:, :128], preferred_element_type=F32)
    logits = logits * scale[:, 0:1]
    shifted = jnp.exp(logits - jnp.max(logits, axis=1, keepdims=True))
    unit = float(fine) / jnp.sum(shifted, axis=1, keepdims=True)
    return (shifted * unit).astype(BF)


def copy_body(x, out):
    out[...] = x[...]


def halve(values, outs):
    size = values.shape[0] // len(outs)
    for n, out in enumerate(outs):
        out[...] = values[n * size : (n + 1) * size, :]


def soft_body(rows, count, block, *refs):
    outs = refs[count:]
    halve(soft_rows(block, rows, 0, refs[:count], outs[0].shape[1]), outs)


def softs_body(rows, count, order, blocks, *refs):
    outs = refs[count:]
    each = len(outs) // len(order)
    step = rows + META

    def one(n, _):
        k = 0
        for m, number in enumerate(order):
            k = jnp.where(n == m, number, k)
        block = blocks[pl.ds(pl.multiple_of(k * step, 16), step), :]
        values = soft_rows(block, rows, 0, refs[:count], outs[0].shape[1])
        for m in range(len(order)):

            @pl.when(n == m)
            def _(m=m):
                halve(values, outs[m * each : (m + 1) * each])

        return 0

    lax.fori_loop(0, len(order), one, 0)


def other_body(groups, rows, blocks, *refs):
    out = refs[-1]
    step = rows + META

    def one(k, _):
        block = blocks[pl.ds(pl.multiple_of(k * step, 16), step), :]
        values = soft_rows(block, rows, 4, refs[:-1], out.shape[1])
        out[pl.ds(pl.multiple_of(k * rows, 16), rows), :] = values
        return 0

    lax.fori_loop(0, groups, one, 0)


def sums(rows, first, blocks, pieces, across, put):
    width = blocks.shape[1]
    step = rows + META
    count = blocks.shape[0] // step
    lane = lax.broadcasted_iota(jnp.int32, (1, width), 1)
    row = lax.broadcasted_iota(jnp.int32, (rows, 1), 0).astype(F32)
    start = 0
    for ref in pieces:
        across[:, start : start + ref.shape[0]] = ref[...].T
        start += ref.shape[0]

    def one(c, _):
        chosen = []
        for n in range(count):
            bounds = blocks[n * step + rows : (n + 1) * step, :].astype(F32)
            ends = jnp.sum(jnp.where(lane == 128 + c + first, bounds, 0.0), axis=1, keepdims=True)
            inside = (row >= ends[0:1, :]) & (row < ends[1:2, :])
            chosen.append(blocks[n * step : n * step + rows, :] * inside.astype(F32).astype(BF))
        put(c, jnp.dot(across[...], jnp.concatenate(chosen, axis=0), preferred_element_type=F32))
        return 0

    lax.fori_loop(0, 4, one, 0)
    members = []
    for n in range(count):
        ends = blocks[n * step + rows : (n + 1) * step, :].astype(F32)[:, 128:256]
        members.append(((row >= ends[0:1, :]) & (row < ends[1:2, :])).astype(F32).astype(BF))
    masses = jnp.dot(across[...], jnp.concatenate(members, axis=0), preferred_element_type=F32).T
    return masses[first : first + 4, :]


def here_body(rows, blocks, *refs):
    *pieces, out, mass_out, across = refs

    def put(c, value):
        out[c] = value

    mass_out[...] = sums(rows, 0, blocks, pieces, across, put)


def sums_body(rows, others, soft, centres, before, mass_before, out, mass_out, give, across, total):
    width = others.shape[1]
    fine = soft.shape[1]
    count = fine // width

    def put(c, value):
        total[c] = before[c] + value

    masses = mass_before[...] + sums(rows, 4, others, [soft], across, put)
    for n in range(2):
        out[n] = total[n] + centres[n].astype(F32)
        give[n, :fine, :] = total[2 + n].astype(BF)
        own, other = [
            jnp.concatenate([masses[m : m + 1, q * width : (q + 1) * width] for q in range(count)], axis=0)
            for m in (n, 2 + n)
        ]
        mass_out[n] = own + 1.0
        terms = [t.astype(F32) for t in three(other)]
        rest = jnp.zeros((META - 3 * count, width), F32)
        give[n, fine:, :] = jnp.concatenate(terms + [rest], axis=0).astype(BF)


def unpack_body(starts, slot, *refs):
    *refs, out = refs
    frames, fine = out.shape
    picks = []
    for start, ref in zip(starts, refs):
        lane = lax.broadcasted_iota(jnp.int32, (frames, ref.shape[0]), 1)
        picks.append((slot[...] == lane + start).astype(F32).astype(BF))
    pick = jnp.concatenate(picks, axis=1)
    width = 256
    for q in range(fine // width):
        span = slice(q * width, (q + 1) * width)
        values = jnp.concatenate([ref[:, span] for ref in refs], axis=0)
        out[:, span] = jnp.dot(pick, values, preferred_element_type=F32).astype(BF)


def finish_body(mine, mass, got, out):
    fine, width = out.shape[1:]
    spans = fine // width
    for n in range(out.shape[0]):
        tail = got[n, fine:, :].astype(F32)
        total = mass[n]
        for t in range(3):
            total = total + tail[t * spans : (t + 1) * spans, :]
        inverse = 1.0 / total
        for q in range(spans):
            column = jnp.broadcast_to(inverse[q : q + 1, :], (8, width)).T[:, 0:1]
            span = slice(q * width, (q + 1) * width)
            out[n, span, :] = (mine[n, span, :] + got[n, span, :].astype(F32)) * column


def shards(codes, labels, centroids, sharpness):
    route = lax.axis_size("route")
    frames, width = codes.shape
    per_device, fine, _ = centroids.shape
    groups = route // GRP
    rows = GRP * max(8, 2 * frames // route)
    def turn(x, distance, places=range(groups)):
        pairs = [(GRP * g + m, GRP * (g ^ distance) + m) for g in places for m in range(GRP)]
        return lax.ppermute(x, "route", pairs)

    here = lax.axis_index("route").astype(jnp.int32).reshape(1)

    def swap(x, mask):
        return lax.ppermute(x, "route", [(r, r ^ mask) for r in range(route)])

    sharp = sharpness.reshape(per_device, 1)
    own, far = [], []
    for c in range(per_device):
        own.append(
            call(
                functools.partial(share_body, c),
                jax.ShapeDtypeStruct((fine + 8 * (fine // width), width), BF),
                2,
                SCALE * 4 * 8 * fine * width,
                SCALE * fine * width * 4,
                in_specs=[VMEM, pl.BlockSpec(memory_space=pl.ANY)],
                scratch=[pltpu.SemaphoreType.DMA],
            )(sharp, centroids)
        )
        far.append(swap(own[c], 2))
    here, _ = lax.optimization_barrier((here, own[0]))
    block_shape = jax.ShapeDtypeStruct((rows + META, width), BF)
    *send, slot = call(
        functools.partial(pack_body, groups, rows),
        [block_shape] * groups + [jax.ShapeDtypeStruct((frames, 1), jnp.int32)],
        3,
        SCALE * 2 * groups * rows * frames * width,
        SCALE * frames * width * 8,
        in_specs=[SMEM, VMEM, VMEM],
    )(here, labels.reshape(1, frames), codes)
    *send, _ = lax.optimization_barrier((*send, own[1]))
    blocks = {0: send[0]}
    for k in range(1, groups):
        blocks[k] = turn(send[k], k)
    arrived = [blocks[k] for k in range(1, groups)]
    busy = here
    if groups == 4:
        busy = call(
            functools.partial(busy_body, groups, rows),
            jax.ShapeDtypeStruct((1,), jnp.int32),
            1 + groups,
            1000,
            1000,
            in_specs=[SMEM] + [VMEM] * groups,
            out_specs=SMEM,
        )(here, *[blocks[k] for k in range(groups)])
    near = [swap(lax.optimization_barrier((x, *arrived))[0], 1) for x in own]
    last = [swap(lax.optimization_barrier((x, busy, *arrived))[0], 1) for x in far]

    halves = 2 if groups == 4 else 1
    work = 2 * rows * fine * width * 2 * GRP
    held = [call(copy_body, jax.ShapeDtypeStruct(x.shape, BF), 1, 0, 0)(x) for x in (*own, *near, *far, *last)]
    half = jax.ShapeDtypeStruct((rows // halves, fine), BF)
    early = [1, 2] if groups > 2 else [1]
    late = [k for k in range(groups - 1, -1, -1) if k not in early]
    first = [
        call(
            functools.partial(soft_body, rows, len(held)),
            [half] * halves if k > 1 else [jax.ShapeDtypeStruct((rows, fine), BF)],
            1 + len(held),
            SCALE * work,
            SCALE * GRP * per_device * fine * width * 2,
        )(blocks[k], *held)
        for k in early[:1]
    ]

    def refine(places, first, held, gathered, slot, centroids):
        others = swap(gathered, 2)
        out = call(
            functools.partial(softs_body, rows, len(held), late),
            [half] * (halves * len(late)),
            1 + len(held),
            SCALE * len(late) * work,
            SCALE * GRP * per_device * fine * width * 2,
        )(gathered, *held)
        soft = dict(zip(early, first))
        for k in early[1:]:
            soft[k] = call(
                functools.partial(soft_body, rows, len(held)),
                [half] * halves,
                1 + len(held),
                SCALE * work,
                SCALE * GRP * per_device * fine * width * 2,
            )(gathered[k * (rows + META) : (k + 1) * (rows + META)], *held)
        for n, k in enumerate(late):
            soft[k] = out[n * halves : (n + 1) * halves]
        back = dict(soft)
        for k in early + late:
            if k:
                back[k] = [turn(soft[k][0], k)] + [turn(x, k, places) for x in soft[k][1:]]
        sums_shape = ((2 * per_device, fine, width), F32)
        across = ((fine, groups * rows), BF)
        work_sums = LIGHT * 8 * groups * rows * fine * width
        before, mass_before = call(
            functools.partial(here_body, rows),
            [jax.ShapeDtypeStruct(*sums_shape), jax.ShapeDtypeStruct((2 * per_device, fine), F32)],
            1 + sum(len(soft[k]) for k in range(groups)),
            work_sums,
            LIGHT * groups * rows * fine * 4,
            scratch=[across],
        )(gathered, *[x for k in range(groups) for x in soft[k]])
        others, mass_before = lax.optimization_barrier((others, mass_before))
        other_soft = call(
            functools.partial(other_body, groups, rows),
            jax.ShapeDtypeStruct((groups * rows, fine), BF),
            1 + 2 * per_device,
            0,
            0,
        )(others, *held[: 2 * per_device])
        if groups > 2:
            other_soft, back[2] = lax.optimization_barrier((other_soft, back[2]))
        mine, mass, give = call(
            functools.partial(sums_body, rows),
            [
                jax.ShapeDtypeStruct(centroids.shape, F32),
                jax.ShapeDtypeStruct((per_device, fine // width, width), F32),
                jax.ShapeDtypeStruct((per_device, fine + META, width), BF),
            ],
            5,
            work_sums,
            LIGHT * groups * rows * fine * 4,
            scratch=[across, sums_shape],
        )(others, other_soft, centroids, before, mass_before)
        got = swap(give, 1)
        pieces = []
        for k in range(groups):
            size = rows // len(back[k])
            pieces += [(k * rows + n * size, x) for n, x in enumerate(back[k])]
        soft_labels = call(
            functools.partial(unpack_body, [start for start, _ in pieces]),
            jax.ShapeDtypeStruct((slot.shape[0], fine), BF),
            1 + len(pieces),
            HEAVY * slot.shape[0] * groups * rows * fine,
            HEAVY * groups * rows * fine * 2,
        )(slot, *[x for _, x in pieces])
        new_centroids = call(
            finish_body,
            jax.ShapeDtypeStruct(centroids.shape, F32),
            3,
            4 * per_device * fine * width,
            per_device * fine * width * 10,
        )(mine, mass, got)
        return soft_labels, new_centroids

    gathered = jnp.concatenate([blocks[k] for k in range(groups)], axis=0)
    shared = (first, held, gathered, slot, centroids)
    if halves == 1:
        return refine(range(groups), *shared)
    cases = [functools.partial(refine, c) for c in ((0, 3), (1, 2), range(groups))]
    return lax.switch(busy[0], cases, *shared)


def solution(mesh):
    placed = (
        P(("parts", "route"), None),
        P(("parts", "route")),
        P(("parts", "route"), None, None),
        P(("parts", "route")),
    )
    return jax.shard_map(
        shards,
        mesh=mesh,
        in_specs=placed,
        out_specs=(P(("parts", "route"), None), P(("parts", "route"), None, None)),
        check_vma=False,
    )
```

```python
import functools

import jax
import jax.numpy as jnp
from jax import lax
from jax.experimental import pallas as pl
from jax.experimental.pallas import tpu as pltpu
from jax.sharding import PartitionSpec as P

GRP = 4
META = 16
SCALE = 5
LIGHT = 1
HEAVY = 100
BF = jnp.bfloat16
F32 = jnp.float32
VMEM = pl.BlockSpec(memory_space=pltpu.VMEM)
SMEM = pl.BlockSpec(memory_space=pltpu.SMEM)


def call(body, out_shape, n_in, flops, nbytes, in_specs=None, out_specs=None, scratch=()):
    many = isinstance(out_shape, (list, tuple))
    return pl.pallas_call(
        body,
        out_shape=out_shape,
        in_specs=in_specs or [VMEM] * n_in,
        out_specs=out_specs or ([VMEM] * len(out_shape) if many else VMEM),
        scratch_shapes=[pltpu.VMEM(*x) if isinstance(x, tuple) else x for x in scratch],
        compiler_params=pltpu.CompilerParams(vmem_limit_bytes=24 * 1024 * 1024),
        cost_estimate=pl.CostEstimate(flops=flops, bytes_accessed=nbytes, transcendentals=0),
    )


def three(value):
    first = value.astype(BF)
    rest = value - first.astype(F32)
    second = rest.astype(BF)
    third = (rest - second.astype(F32)).astype(BF)
    return first, second, third


def cluster_lanes(shape):
    lane = lax.broadcasted_iota(jnp.int32, shape, 1)
    return jnp.where(lane < 128, lane >> 4, lane - 128)


def pack_body(groups, rows, here, labels, codes, *outs):
    frames, width = codes.shape
    group, place = here[0] // GRP, here[0] % GRP
    kr = jnp.broadcast_to(labels[...], (8, frames)) ^ (group * 8 + place * 2)
    kc = kr.T[:, 0:1]
    kr = kr[0:1, :]
    lane = lax.broadcasted_iota(jnp.int32, (1, frames), 1)
    sub = lax.broadcasted_iota(jnp.int32, (frames, 1), 0)
    ur, uc = kr * frames + lane, kc * frames + sub
    gr = kr >> 3
    base_r = gr * (8 * frames)
    rank = jnp.sum(((uc < ur) & (uc >= base_r)).astype(jnp.int32), axis=0, keepdims=True)
    slot = gr * rows + rank
    rounded = codes[...].astype(BF)
    target = lax.broadcasted_iota(jnp.int32, (rows, frames), 0)
    cluster = cluster_lanes((1, width))
    row = lax.broadcasted_iota(jnp.int32, (META, width), 0)
    step = lax.broadcasted_iota(jnp.int32, (frames, width), 1)
    counts = jnp.sum(((kc >> 3) == step).astype(F32), axis=0, keepdims=True)
    for k in range(groups):
        pick = (slot == target + k * rows).astype(F32).astype(BF)
        outs[k][:rows, :] = jnp.dot(pick, rounded, preferred_element_type=F32).astype(BF)
        inside = kc >= 8 * k
        first = jnp.sum((inside & (kc < 8 * k + cluster)).astype(F32), axis=0, keepdims=True)
        last = jnp.sum((inside & (kc < 8 * k + cluster + 1)).astype(F32), axis=0, keepdims=True)
        bounds = jnp.where(row == 0, first, jnp.where(row == 1, last, jnp.where(row == 2, counts, 0.0)))
        outs[k][rows:, :] = bounds.astype(BF)
    gc = kc >> 3
    base_c = gc * (8 * frames)
    rank_c = jnp.sum(((ur < uc) & (ur >= base_c)).astype(jnp.int32), axis=1, keepdims=True)
    outs[groups][...] = gc * rows + rank_c


def first_rows(rows):
    return rows * 7 // 16 // 16 * 16


def busy_body(groups, rows, here, *refs):
    out = refs[groups]
    lane = lax.broadcasted_iota(jnp.int32, (1, refs[0].shape[1]), 1)
    group = here[0] // GRP
    flags = [0, 0]
    for d in range(groups):
        most = jnp.zeros(lane.shape, F32)
        for s in range(groups):
            counts = refs[s][rows:, :].astype(F32)[2:3, :]
            most = jnp.maximum(most, jnp.where(lane == d ^ s, counts, 0.0))
        flag = (jnp.max(most) > float(first_rows(rows))).astype(jnp.int32)
        side = (d ^ (d >> 1)) & 1
        flags[side] = flags[side] | flag
    between = (group ^ (group >> 1)) & 1
    same, other = flags
    outer = jnp.where(between == 0, same, other)
    inner = jnp.where(between == 0, other, same)
    out[0] = jnp.where(inner == 0, 0, jnp.where(outer == 0, 1, 2))


def share_body(c, sharp, centres, out, sem):
    width = out.shape[1]
    fine = centres.shape[1]
    copy = pltpu.make_async_copy(centres.at[c], out.at[pl.ds(0, fine)], sem)
    copy.start()
    copy.wait()
    row = lax.broadcasted_iota(jnp.int32, (8, width), 0)
    ones = jnp.ones((8, width), BF)
    dims = (((1,), (1,)), ((), ()))
    values = out[:fine, :]
    wide = values.astype(F32)
    square = wide * wide
    high = square.astype(BF)
    low = (square - high.astype(F32)).astype(BF)
    norm = lax.dot_general(ones, high, dims, preferred_element_type=F32)
    norm = norm + lax.dot_general(ones, low, dims, preferred_element_type=F32)
    terms = [t.astype(F32) for t in three(-0.5 * norm)]
    tiles = []
    for q in range(fine // width):
        tile = jnp.where(row == 3, sharp[c : c + 1, 0:1].astype(F32), 0.0)
        for t in range(3):
            tile = jnp.where(row == t, terms[t][:, q * width : (q + 1) * width], tile)
        tiles.append(tile)
    out[fine:, :] = jnp.concatenate(tiles, axis=0).astype(BF)


def member_lanes(block, rows):
    bounds = block[rows:, :].astype(F32)
    row = lax.broadcasted_iota(jnp.int32, (rows, block.shape[1]), 0).astype(F32)
    return ((row >= bounds[0:1, :]) & (row < bounds[1:2, :])).astype(F32)


def mass_rows(row, mass):
    terms = three(mass)
    total = jnp.zeros(row.shape, F32)
    for t in range(3):
        total = jnp.where(row == t, terms[t].astype(F32), total)
    return total.astype(BF)


def soft_rows(block, rows, first, refs, fine):
    member = member_lanes(block, rows).astype(BF)
    codes = block[:rows, :]
    count = len(refs)
    width = codes.shape[1]
    pick = member[:, 16 * first : 16 * (first + count)]
    part = lax.broadcasted_iota(jnp.int32, pick.shape, 1) & 15
    zero = jnp.zeros_like(pick)
    low = jnp.where(part < 3, pick, zero)
    high = jnp.where((part >= 8) & (part < 11), pick, zero)
    columns = []
    for q in range(0, fine // width, 2):
        start = fine + 8 * q
        table = jnp.concatenate([ref[start : start + 16, :] for ref in refs], axis=0)
        columns += [jnp.dot(p, table, preferred_element_type=F32) for p in (low, high)]
    logits = jnp.concatenate(columns, axis=1)
    for n, ref in enumerate(refs):
        r = first + n
        chosen = codes * member[:, 128 + r : 129 + r]
        logits = logits + lax.dot_general(
            chosen, ref[:fine, :], (((1,), (1,)), ((), ())), preferred_element_type=F32
        )
    scale = jnp.dot(jnp.where(part == 3, pick, zero), table[:, :128], preferred_element_type=F32)
    logits = logits * scale[:, 0:1]
    shifted = jnp.exp(logits - jnp.max(logits, axis=1, keepdims=True))
    unit = float(fine) / jnp.sum(shifted, axis=1, keepdims=True)
    return (shifted * unit).astype(BF)


def copy_body(x, out):
    out[...] = x[...]


def halve(values, outs):
    start = 0
    for out in outs:
        out[...] = values[start : start + out.shape[0], :]
        start += out.shape[0]


def soft_body(rows, count, block, *refs):
    outs = refs[count:]
    halve(soft_rows(block, rows, 0, refs[:count], outs[0].shape[1]), outs)


def softs_body(rows, count, order, blocks, *refs):
    outs = refs[count:]
    each = len(outs) // len(order)
    step = rows + META

    def one(n, _):
        k = 0
        for m, number in enumerate(order):
            k = jnp.where(n == m, number, k)
        block = blocks[pl.ds(pl.multiple_of(k * step, 16), step), :]
        values = soft_rows(block, rows, 0, refs[:count], outs[0].shape[1])
        for m in range(len(order)):

            @pl.when(n == m)
            def _(m=m):
                halve(values, outs[m * each : (m + 1) * each])

        return 0

    lax.fori_loop(0, len(order), one, 0)


def other_body(groups, rows, blocks, *refs):
    out = refs[-1]
    step = rows + META

    def one(k, _):
        block = blocks[pl.ds(pl.multiple_of(k * step, 16), step), :]
        values = soft_rows(block, rows, 4, refs[:-1], out.shape[1])
        out[pl.ds(pl.multiple_of(k * rows, 16), rows), :] = values
        return 0

    lax.fori_loop(0, groups, one, 0)


def sums(rows, first, blocks, pieces, across, put):
    width = blocks.shape[1]
    step = rows + META
    count = blocks.shape[0] // step
    lane = lax.broadcasted_iota(jnp.int32, (1, width), 1)
    row = lax.broadcasted_iota(jnp.int32, (rows, 1), 0).astype(F32)
    start = 0
    for ref in pieces:
        across[:, start : start + ref.shape[0]] = ref[...].T
        start += ref.shape[0]

    def one(c, _):
        chosen = []
        for n in range(count):
            bounds = blocks[n * step + rows : (n + 1) * step, :].astype(F32)
            ends = jnp.sum(jnp.where(lane == 128 + c + first, bounds, 0.0), axis=1, keepdims=True)
            inside = (row >= ends[0:1, :]) & (row < ends[1:2, :])
            chosen.append(blocks[n * step : n * step + rows, :] * inside.astype(F32).astype(BF))
        put(c, jnp.dot(across[...], jnp.concatenate(chosen, axis=0), preferred_element_type=F32))
        return 0

    lax.fori_loop(0, 4, one, 0)
    members = []
    for n in range(count):
        ends = blocks[n * step + rows : (n + 1) * step, :].astype(F32)[:, 128:256]
        members.append(((row >= ends[0:1, :]) & (row < ends[1:2, :])).astype(F32).astype(BF))
    masses = jnp.dot(across[...], jnp.concatenate(members, axis=0), preferred_element_type=F32).T
    return masses[first : first + 4, :]


def here_body(rows, blocks, *refs):
    *pieces, out, mass_out, across = refs

    def put(c, value):
        out[c] = value

    mass_out[...] = sums(rows, 0, blocks, pieces, across, put)


def sums_body(rows, others, soft, centres, before, mass_before, out, mass_out, give, across, total):
    width = others.shape[1]
    fine = soft.shape[1]
    count = fine // width

    def put(c, value):
        total[c] = before[c] + value

    masses = mass_before[...] + sums(rows, 4, others, [soft], across, put)
    for n in range(2):
        out[n] = total[n] + centres[n].astype(F32)
        give[n, :fine, :] = total[2 + n].astype(BF)
        own, other = [
            jnp.concatenate([masses[m : m + 1, q * width : (q + 1) * width] for q in range(count)], axis=0)
            for m in (n, 2 + n)
        ]
        mass_out[n] = own + 1.0
        terms = [t.astype(F32) for t in three(other)]
        rest = jnp.zeros((META - 3 * count, width), F32)
        give[n, fine:, :] = jnp.concatenate(terms + [rest], axis=0).astype(BF)


def unpack_body(starts, slot, *refs):
    *refs, out = refs
    frames, fine = out.shape
    picks = []
    for start, ref in zip(starts, refs):
        lane = lax.broadcasted_iota(jnp.int32, (frames, ref.shape[0]), 1)
        picks.append((slot[...] == lane + start).astype(F32).astype(BF))
    pick = jnp.concatenate(picks, axis=1)
    width = 256
    for q in range(fine // width):
        span = slice(q * width, (q + 1) * width)
        values = jnp.concatenate([ref[:, span] for ref in refs], axis=0)
        out[:, span] = jnp.dot(pick, values, preferred_element_type=F32).astype(BF)


def finish_body(mine, mass, got, out):
    fine, width = out.shape[1:]
    spans = fine // width
    for n in range(out.shape[0]):
        tail = got[n, fine:, :].astype(F32)
        total = mass[n]
        for t in range(3):
            total = total + tail[t * spans : (t + 1) * spans, :]
        inverse = 1.0 / total
        for q in range(spans):
            column = jnp.broadcast_to(inverse[q : q + 1, :], (8, width)).T[:, 0:1]
            span = slice(q * width, (q + 1) * width)
            out[n, span, :] = (mine[n, span, :] + got[n, span, :].astype(F32)) * column


def shards(codes, labels, centroids, sharpness):
    route = lax.axis_size("route")
    frames, width = codes.shape
    per_device, fine, _ = centroids.shape
    groups = route // GRP
    rows = GRP * max(8, 2 * frames // route)
    def turn(x, distance, places=range(groups)):
        pairs = [(GRP * g + m, GRP * (g ^ distance) + m) for g in places for m in range(GRP)]
        return lax.ppermute(x, "route", pairs)

    here = lax.axis_index("route").astype(jnp.int32).reshape(1)

    def swap(x, mask):
        return lax.ppermute(x, "route", [(r, r ^ mask) for r in range(route)])

    sharp = sharpness.reshape(per_device, 1)
    own, far = [], []
    for c in range(per_device):
        own.append(
            call(
                functools.partial(share_body, c),
                jax.ShapeDtypeStruct((fine + 8 * (fine // width), width), BF),
                2,
                SCALE * 4 * 8 * fine * width,
                SCALE * fine * width * 4,
                in_specs=[VMEM, pl.BlockSpec(memory_space=pl.ANY)],
                scratch=[pltpu.SemaphoreType.DMA],
            )(sharp, centroids)
        )
        far.append(swap(own[c], 2))
    here, _ = lax.optimization_barrier((here, own[0]))
    block_shape = jax.ShapeDtypeStruct((rows + META, width), BF)
    *send, slot = call(
        functools.partial(pack_body, groups, rows),
        [block_shape] * groups + [jax.ShapeDtypeStruct((frames, 1), jnp.int32)],
        3,
        SCALE * 2 * groups * rows * frames * width,
        SCALE * frames * width * 8,
        in_specs=[SMEM, VMEM, VMEM],
    )(here, labels.reshape(1, frames), codes)
    *send, _ = lax.optimization_barrier((*send, own[1]))
    blocks = {0: send[0]}
    for k in range(1, groups):
        blocks[k] = turn(send[k], k)
    arrived = [blocks[k] for k in range(1, groups)]
    busy = here
    if groups == 4:
        busy = call(
            functools.partial(busy_body, groups, rows),
            jax.ShapeDtypeStruct((1,), jnp.int32),
            1 + groups,
            1000,
            1000,
            in_specs=[SMEM] + [VMEM] * groups,
            out_specs=SMEM,
        )(here, *[blocks[k] for k in range(groups)])
    near = [swap(lax.optimization_barrier((x, *arrived))[0], 1) for x in own]
    last = [swap(lax.optimization_barrier((x, busy, *arrived))[0], 1) for x in far]

    halves = 2 if groups == 4 else 1
    work = 2 * rows * fine * width * 2 * GRP
    held = [call(copy_body, jax.ShapeDtypeStruct(x.shape, BF), 1, 0, 0)(x) for x in (*own, *near, *far, *last)]
    sizes = [first_rows(rows), rows - first_rows(rows)] if halves > 1 else [rows]
    half = [jax.ShapeDtypeStruct((size, fine), BF) for size in sizes]
    early = [1, 2] if groups > 2 else [1]
    late = [k for k in range(groups - 1, -1, -1) if k not in early]
    first = [
        call(
            functools.partial(soft_body, rows, len(held)),
            half if k > 1 else [jax.ShapeDtypeStruct((rows, fine), BF)],
            1 + len(held),
            SCALE * work,
            SCALE * GRP * per_device * fine * width * 2,
        )(blocks[k], *held)
        for k in early[:1]
    ]

    def refine(places, first, held, gathered, slot, centroids):
        others = swap(gathered, 2)
        out = call(
            functools.partial(softs_body, rows, len(held), late),
            half * len(late),
            1 + len(held),
            SCALE * len(late) * work,
            SCALE * GRP * per_device * fine * width * 2,
        )(gathered, *held)
        soft = dict(zip(early, first))
        for k in early[1:]:
            soft[k] = call(
                functools.partial(soft_body, rows, len(held)),
                half,
                1 + len(held),
                SCALE * work,
                SCALE * GRP * per_device * fine * width * 2,
            )(gathered[k * (rows + META) : (k + 1) * (rows + META)], *held)
        for n, k in enumerate(late):
            soft[k] = out[n * halves : (n + 1) * halves]
        back = dict(soft)
        for k in early + late:
            if k:
                back[k] = [turn(soft[k][0], k)] + [turn(x, k, places) for x in soft[k][1:]]
        sums_shape = ((2 * per_device, fine, width), F32)
        across = ((fine, groups * rows), BF)
        work_sums = LIGHT * 8 * groups * rows * fine * width
        before, mass_before = call(
            functools.partial(here_body, rows),
            [jax.ShapeDtypeStruct(*sums_shape), jax.ShapeDtypeStruct((2 * per_device, fine), F32)],
            1 + sum(len(soft[k]) for k in range(groups)),
            work_sums,
            LIGHT * groups * rows * fine * 4,
            scratch=[across],
        )(gathered, *[x for k in range(groups) for x in soft[k]])
        others, mass_before = lax.optimization_barrier((others, mass_before))
        other_soft = call(
            functools.partial(other_body, groups, rows),
            jax.ShapeDtypeStruct((groups * rows, fine), BF),
            1 + 2 * per_device,
            0,
            0,
        )(others, *held[: 2 * per_device])
        if groups > 2:
            other_soft, back[2] = lax.optimization_barrier((other_soft, back[2]))
        mine, mass, give = call(
            functools.partial(sums_body, rows),
            [
                jax.ShapeDtypeStruct(centroids.shape, F32),
                jax.ShapeDtypeStruct((per_device, fine // width, width), F32),
                jax.ShapeDtypeStruct((per_device, fine + META, width), BF),
            ],
            5,
            work_sums,
            LIGHT * groups * rows * fine * 4,
            scratch=[across, sums_shape],
        )(others, other_soft, centroids, before, mass_before)
        got = swap(give, 1)
        pieces = []
        for k in range(groups):
            start = k * rows
            for x in back[k]:
                pieces.append((start, x))
                start += x.shape[0]
        soft_labels = call(
            functools.partial(unpack_body, [start for start, _ in pieces]),
            jax.ShapeDtypeStruct((slot.shape[0], fine), BF),
            1 + len(pieces),
            HEAVY * slot.shape[0] * groups * rows * fine,
            HEAVY * groups * rows * fine * 2,
        )(slot, *[x for _, x in pieces])
        new_centroids = call(
            finish_body,
            jax.ShapeDtypeStruct(centroids.shape, F32),
            3,
            4 * per_device * fine * width,
            per_device * fine * width * 10,
        )(mine, mass, got)
        return soft_labels, new_centroids

    gathered = jnp.concatenate([blocks[k] for k in range(groups)], axis=0)
    shared = (first, held, gathered, slot, centroids)
    if halves == 1:
        return refine(range(groups), *shared)
    cases = [functools.partial(refine, c) for c in ((0, 3), (1, 2), range(groups))]
    return lax.switch(busy[0], cases, *shared)


def solution(mesh):
    placed = (
        P(("parts", "route"), None),
        P(("parts", "route")),
        P(("parts", "route"), None, None),
        P(("parts", "route")),
    )
    return jax.shard_map(
        shards,
        mesh=mesh,
        in_specs=placed,
        out_specs=(P(("parts", "route"), None), P(("parts", "route"), None, None)),
        check_vma=False,
    )
```

```python
import functools

import jax
import jax.numpy as jnp
from jax import lax
from jax.experimental import pallas as pl
from jax.experimental.pallas import tpu as pltpu
from jax.sharding import PartitionSpec as P

GRP = 4
META = 16
SCALE = 5
LIGHT = 1
HEAVY = 100
BF = jnp.bfloat16
F32 = jnp.float32
VMEM = pl.BlockSpec(memory_space=pltpu.VMEM)
SMEM = pl.BlockSpec(memory_space=pltpu.SMEM)


def call(body, out_shape, n_in, flops, nbytes, in_specs=None, out_specs=None, scratch=()):
    many = isinstance(out_shape, (list, tuple))
    return pl.pallas_call(
        body,
        out_shape=out_shape,
        in_specs=in_specs or [VMEM] * n_in,
        out_specs=out_specs or ([VMEM] * len(out_shape) if many else VMEM),
        scratch_shapes=[pltpu.VMEM(*x) if isinstance(x, tuple) else x for x in scratch],
        compiler_params=pltpu.CompilerParams(vmem_limit_bytes=24 * 1024 * 1024),
        cost_estimate=pl.CostEstimate(flops=flops, bytes_accessed=nbytes, transcendentals=0),
    )


def three(value):
    first = value.astype(BF)
    rest = value - first.astype(F32)
    second = rest.astype(BF)
    third = (rest - second.astype(F32)).astype(BF)
    return first, second, third


def cluster_lanes(shape):
    lane = lax.broadcasted_iota(jnp.int32, shape, 1)
    return jnp.where(lane < 128, lane >> 4, lane - 128)


def pack_body(groups, rows, here, labels, codes, *outs):
    frames, width = codes.shape
    group, place = here[0] // GRP, here[0] % GRP
    kr = jnp.broadcast_to(labels[...], (8, frames)) ^ (group * 8 + place * 2)
    kc = kr.T[:, 0:1]
    kr = kr[0:1, :]
    lane = lax.broadcasted_iota(jnp.int32, (1, frames), 1)
    sub = lax.broadcasted_iota(jnp.int32, (frames, 1), 0)
    ur, uc = kr * frames + lane, kc * frames + sub
    gr = kr >> 3
    base_r = gr * (8 * frames)
    rank = jnp.sum(((uc < ur) & (uc >= base_r)).astype(jnp.int32), axis=0, keepdims=True)
    slot = gr * rows + rank
    rounded = codes[...].astype(BF)
    target = lax.broadcasted_iota(jnp.int32, (rows, frames), 0)
    cluster = cluster_lanes((1, width))
    row = lax.broadcasted_iota(jnp.int32, (META, width), 0)
    step = lax.broadcasted_iota(jnp.int32, (frames, width), 1)
    counts = jnp.sum(((kc >> 3) == step).astype(F32), axis=0, keepdims=True)
    for k in range(groups):
        pick = (slot == target + k * rows).astype(F32).astype(BF)
        outs[k][:rows, :] = jnp.dot(pick, rounded, preferred_element_type=F32).astype(BF)
        inside = kc >= 8 * k
        first = jnp.sum((inside & (kc < 8 * k + cluster)).astype(F32), axis=0, keepdims=True)
        last = jnp.sum((inside & (kc < 8 * k + cluster + 1)).astype(F32), axis=0, keepdims=True)
        bounds = jnp.where(row == 0, first, jnp.where(row == 1, last, jnp.where(row == 2, counts, 0.0)))
        outs[k][rows:, :] = bounds.astype(BF)
    gc = kc >> 3
    base_c = gc * (8 * frames)
    rank_c = jnp.sum(((ur < uc) & (ur >= base_c)).astype(jnp.int32), axis=1, keepdims=True)
    outs[groups][...] = gc * rows + rank_c


def first_rows(rows):
    return rows * 7 // 16 // 16 * 16


def busy_body(groups, rows, here, *refs):
    out = refs[groups]
    lane = lax.broadcasted_iota(jnp.int32, (1, refs[0].shape[1]), 1)
    group = here[0] // GRP
    flags = [0, 0]
    for d in range(groups):
        most = jnp.zeros(lane.shape, F32)
        for s in range(groups):
            counts = refs[s][rows:, :].astype(F32)[2:3, :]
            most = jnp.maximum(most, jnp.where(lane == d ^ s, counts, 0.0))
        flag = (jnp.max(most) > float(first_rows(rows))).astype(jnp.int32)
        side = (d ^ (d >> 1)) & 1
        flags[side] = flags[side] | flag
    between = (group ^ (group >> 1)) & 1
    same, other = flags
    outer = jnp.where(between == 0, same, other)
    inner = jnp.where(between == 0, other, same)
    out[0] = jnp.where(inner == 0, 0, jnp.where(outer == 0, 1, 2))


def share_body(c, sharp, centres, out, sem):
    width = out.shape[1]
    fine = centres.shape[1]
    copy = pltpu.make_async_copy(centres.at[c], out.at[pl.ds(0, fine)], sem)
    copy.start()
    copy.wait()
    row = lax.broadcasted_iota(jnp.int32, (8, width), 0)
    ones = jnp.ones((8, width), BF)
    dims = (((1,), (1,)), ((), ()))
    values = out[:fine, :]
    wide = values.astype(F32)
    square = wide * wide
    high = square.astype(BF)
    low = (square - high.astype(F32)).astype(BF)
    norm = lax.dot_general(ones, high, dims, preferred_element_type=F32)
    norm = norm + lax.dot_general(ones, low, dims, preferred_element_type=F32)
    terms = [t.astype(F32) for t in three(-0.5 * norm)]
    tiles = []
    for q in range(fine // width):
        tile = jnp.where(row == 3, sharp[0:1, c : c + 1].astype(F32), 0.0)
        for t in range(3):
            tile = jnp.where(row == t, terms[t][:, q * width : (q + 1) * width], tile)
        tiles.append(tile)
    out[fine:, :] = jnp.concatenate(tiles, axis=0).astype(BF)


def member_lanes(block, rows):
    bounds = block[rows:, :].astype(F32)
    row = lax.broadcasted_iota(jnp.int32, (rows, block.shape[1]), 0).astype(F32)
    return ((row >= bounds[0:1, :]) & (row < bounds[1:2, :])).astype(F32)


def mass_rows(row, mass):
    terms = three(mass)
    total = jnp.zeros(row.shape, F32)
    for t in range(3):
        total = jnp.where(row == t, terms[t].astype(F32), total)
    return total.astype(BF)


def soft_rows(block, rows, first, refs, fine):
    member = member_lanes(block, rows).astype(BF)
    codes = block[:rows, :]
    count = len(refs)
    width = codes.shape[1]
    pick = member[:, 16 * first : 16 * (first + count)]
    part = lax.broadcasted_iota(jnp.int32, pick.shape, 1) & 15
    zero = jnp.zeros_like(pick)
    low = jnp.where(part < 3, pick, zero)
    high = jnp.where((part >= 8) & (part < 11), pick, zero)
    columns = []
    for q in range(0, fine // width, 2):
        start = fine + 8 * q
        table = jnp.concatenate([ref[start : start + 16, :] for ref in refs], axis=0)
        columns += [jnp.dot(p, table, preferred_element_type=F32) for p in (low, high)]
    logits = jnp.concatenate(columns, axis=1)
    for n, ref in enumerate(refs):
        r = first + n
        chosen = codes * member[:, 128 + r : 129 + r]
        logits = logits + lax.dot_general(
            chosen, ref[:fine, :], (((1,), (1,)), ((), ())), preferred_element_type=F32
        )
    scale = jnp.dot(jnp.where(part == 3, pick, zero), table[:, :128], preferred_element_type=F32)
    logits = logits * scale[:, 0:1]
    shifted = jnp.exp(logits - jnp.max(logits, axis=1, keepdims=True))
    unit = float(fine) / jnp.sum(shifted, axis=1, keepdims=True)
    return (shifted * unit).astype(BF)


def copy_body(x, out):
    out[...] = x[...]


def halve(values, outs):
    start = 0
    for out in outs:
        out[...] = values[start : start + out.shape[0], :]
        start += out.shape[0]


def soft_body(rows, count, block, *refs):
    outs = refs[count:]
    halve(soft_rows(block, rows, 0, refs[:count], outs[0].shape[1]), outs)


def softs_body(rows, count, order, blocks, *refs):
    outs = refs[count:]
    each = len(outs) // len(order)
    step = rows + META

    def one(n, _):
        k = 0
        for m, number in enumerate(order):
            k = jnp.where(n == m, number, k)
        block = blocks[pl.ds(pl.multiple_of(k * step, 16), step), :]
        values = soft_rows(block, rows, 0, refs[:count], outs[0].shape[1])
        for m in range(len(order)):

            @pl.when(n == m)
            def _(m=m):
                halve(values, outs[m * each : (m + 1) * each])

        return 0

    lax.fori_loop(0, len(order), one, 0)


def other_body(groups, rows, blocks, *refs):
    out = refs[-1]
    step = rows + META

    def one(k, _):
        block = blocks[pl.ds(pl.multiple_of(k * step, 16), step), :]
        values = soft_rows(block, rows, 4, refs[:-1], out.shape[1])
        out[pl.ds(pl.multiple_of(k * rows, 16), rows), :] = values
        return 0

    lax.fori_loop(0, groups, one, 0)


def sums(rows, first, blocks, pieces, across, put):
    width = blocks.shape[1]
    step = rows + META
    count = blocks.shape[0] // step
    lane = lax.broadcasted_iota(jnp.int32, (1, width), 1)
    row = lax.broadcasted_iota(jnp.int32, (rows, 1), 0).astype(F32)
    start = 0
    for ref in pieces:
        across[:, start : start + ref.shape[0]] = ref[...].T
        start += ref.shape[0]

    def one(c, _):
        chosen = []
        for n in range(count):
            bounds = blocks[n * step + rows : (n + 1) * step, :].astype(F32)
            ends = jnp.sum(jnp.where(lane == 128 + c + first, bounds, 0.0), axis=1, keepdims=True)
            inside = (row >= ends[0:1, :]) & (row < ends[1:2, :])
            chosen.append(blocks[n * step : n * step + rows, :] * inside.astype(F32).astype(BF))
        put(c, jnp.dot(across[...], jnp.concatenate(chosen, axis=0), preferred_element_type=F32))
        return 0

    lax.fori_loop(0, 4, one, 0)
    members = []
    for n in range(count):
        ends = blocks[n * step + rows : (n + 1) * step, :].astype(F32)[:, 128:256]
        members.append(((row >= ends[0:1, :]) & (row < ends[1:2, :])).astype(F32).astype(BF))
    masses = jnp.dot(across[...], jnp.concatenate(members, axis=0), preferred_element_type=F32).T
    return masses[first : first + 4, :]


def here_body(rows, blocks, *refs):
    *pieces, out, mass_out, across = refs

    def put(c, value):
        out[c] = value

    mass_out[...] = sums(rows, 0, blocks, pieces, across, put)


def sums_body(rows, others, soft, centres, before, mass_before, out, mass_out, give, across, total):
    width = others.shape[1]
    fine = soft.shape[1]
    count = fine // width

    def put(c, value):
        total[c] = before[c] + value

    masses = mass_before[...] + sums(rows, 4, others, [soft], across, put)
    for n in range(2):
        out[n] = total[n] + centres[n].astype(F32)
        give[n, :fine, :] = total[2 + n].astype(BF)
        own, other = [
            jnp.concatenate([masses[m : m + 1, q * width : (q + 1) * width] for q in range(count)], axis=0)
            for m in (n, 2 + n)
        ]
        mass_out[n] = own + 1.0
        terms = [t.astype(F32) for t in three(other)]
        rest = jnp.zeros((META - 3 * count, width), F32)
        give[n, fine:, :] = jnp.concatenate(terms + [rest], axis=0).astype(BF)


def unpack_body(starts, slot, *refs):
    *refs, out = refs
    frames, fine = out.shape
    picks = []
    for start, ref in zip(starts, refs):
        lane = lax.broadcasted_iota(jnp.int32, (frames, ref.shape[0]), 1)
        picks.append((slot[...] == lane + start).astype(F32).astype(BF))
    pick = jnp.concatenate(picks, axis=1)
    width = 256
    for q in range(fine // width):
        span = slice(q * width, (q + 1) * width)
        values = jnp.concatenate([ref[:, span] for ref in refs], axis=0)
        out[:, span] = jnp.dot(pick, values, preferred_element_type=F32).astype(BF)


def finish_body(mine, mass, got, out):
    fine, width = out.shape[1:]
    spans = fine // width
    for n in range(out.shape[0]):
        tail = got[n, fine:, :].astype(F32)
        total = mass[n]
        for t in range(3):
            total = total + tail[t * spans : (t + 1) * spans, :]
        inverse = 1.0 / total
        for q in range(spans):
            column = jnp.broadcast_to(inverse[q : q + 1, :], (8, width)).T[:, 0:1]
            span = slice(q * width, (q + 1) * width)
            out[n, span, :] = (mine[n, span, :] + got[n, span, :].astype(F32)) * column


def shards(codes, labels, centroids, sharpness):
    route = lax.axis_size("route")
    frames, width = codes.shape
    per_device, fine, _ = centroids.shape
    groups = route // GRP
    rows = GRP * max(8, 2 * frames // route)
    def turn(x, distance, places=range(groups)):
        pairs = [(GRP * g + m, GRP * (g ^ distance) + m) for g in places for m in range(GRP)]
        return lax.ppermute(x, "route", pairs)

    here = lax.axis_index("route").astype(jnp.int32).reshape(1)

    def swap(x, mask):
        return lax.ppermute(x, "route", [(r, r ^ mask) for r in range(route)])

    sharp = sharpness.reshape(1, per_device)
    own, far = [], []
    for c in range(per_device):
        own.append(
            call(
                functools.partial(share_body, c),
                jax.ShapeDtypeStruct((fine + 8 * (fine // width), width), BF),
                2,
                SCALE * 4 * 8 * fine * width,
                SCALE * fine * width * 4,
                in_specs=[VMEM, pl.BlockSpec(memory_space=pl.ANY)],
                scratch=[pltpu.SemaphoreType.DMA],
            )(sharp, centroids)
        )
        far.append(swap(own[c], 2))
    here, _ = lax.optimization_barrier((here, own[0]))
    block_shape = jax.ShapeDtypeStruct((rows + META, width), BF)
    *send, slot = call(
        functools.partial(pack_body, groups, rows),
        [block_shape] * groups + [jax.ShapeDtypeStruct((frames, 1), jnp.int32)],
        3,
        SCALE * 2 * groups * rows * frames * width,
        SCALE * frames * width * 8,
        in_specs=[SMEM, VMEM, VMEM],
    )(here, labels.reshape(1, frames), codes)
    *send, _ = lax.optimization_barrier((*send, own[1]))
    blocks = {0: send[0]}
    for k in range(1, groups):
        blocks[k] = turn(send[k], k)
    arrived = [blocks[k] for k in range(1, groups)]
    busy = here
    if groups == 4:
        busy = call(
            functools.partial(busy_body, groups, rows),
            jax.ShapeDtypeStruct((1,), jnp.int32),
            1 + groups,
            1000,
            1000,
            in_specs=[SMEM] + [VMEM] * groups,
            out_specs=SMEM,
        )(here, *[blocks[k] for k in range(groups)])
    near = [swap(lax.optimization_barrier((x, *arrived))[0], 1) for x in own]
    last = [swap(lax.optimization_barrier((x, busy, *arrived))[0], 1) for x in far]

    halves = 2 if groups == 4 else 1
    work = 2 * rows * fine * width * 2 * GRP
    held = [call(copy_body, jax.ShapeDtypeStruct(x.shape, BF), 1, 0, 0)(x) for x in (*own, *near, *far, *last)]
    sizes = [first_rows(rows), rows - first_rows(rows)] if halves > 1 else [rows]
    half = [jax.ShapeDtypeStruct((size, fine), BF) for size in sizes]
    early = [1, 2] if groups > 2 else [1]
    late = [k for k in range(groups - 1, -1, -1) if k not in early]
    first = [
        call(
            functools.partial(soft_body, rows, len(held)),
            half if k > 1 else [jax.ShapeDtypeStruct((rows, fine), BF)],
            1 + len(held),
            SCALE * work,
            SCALE * GRP * per_device * fine * width * 2,
        )(blocks[k], *held)
        for k in early[:1]
    ]

    def refine(places, first, held, gathered, slot, centroids):
        others = swap(gathered, 2)
        out = call(
            functools.partial(softs_body, rows, len(held), late),
            half * len(late),
            1 + len(held),
            SCALE * len(late) * work,
            SCALE * GRP * per_device * fine * width * 2,
        )(gathered, *held)
        soft = dict(zip(early, first))
        for k in early[1:]:
            soft[k] = call(
                functools.partial(soft_body, rows, len(held)),
                half,
                1 + len(held),
                SCALE * work,
                SCALE * GRP * per_device * fine * width * 2,
            )(gathered[k * (rows + META) : (k + 1) * (rows + META)], *held)
        for n, k in enumerate(late):
            soft[k] = out[n * halves : (n + 1) * halves]
        back = dict(soft)
        for k in early + late:
            if k:
                back[k] = [turn(soft[k][0], k)] + [turn(x, k, places) for x in soft[k][1:]]
        sums_shape = ((2 * per_device, fine, width), F32)
        across = ((fine, groups * rows), BF)
        work_sums = LIGHT * 8 * groups * rows * fine * width
        before, mass_before = call(
            functools.partial(here_body, rows),
            [jax.ShapeDtypeStruct(*sums_shape), jax.ShapeDtypeStruct((2 * per_device, fine), F32)],
            1 + sum(len(soft[k]) for k in range(groups)),
            work_sums,
            LIGHT * groups * rows * fine * 4,
            scratch=[across],
        )(gathered, *[x for k in range(groups) for x in soft[k]])
        others, mass_before = lax.optimization_barrier((others, mass_before))
        other_soft = call(
            functools.partial(other_body, groups, rows),
            jax.ShapeDtypeStruct((groups * rows, fine), BF),
            1 + 2 * per_device,
            0,
            0,
        )(others, *held[: 2 * per_device])
        if groups > 2:
            other_soft, back[2] = lax.optimization_barrier((other_soft, back[2]))
        mine, mass, give = call(
            functools.partial(sums_body, rows),
            [
                jax.ShapeDtypeStruct(centroids.shape, F32),
                jax.ShapeDtypeStruct((per_device, fine // width, width), F32),
                jax.ShapeDtypeStruct((per_device, fine + META, width), BF),
            ],
            5,
            work_sums,
            LIGHT * groups * rows * fine * 4,
            scratch=[across, sums_shape],
        )(others, other_soft, centroids, before, mass_before)
        got = swap(give, 1)
        pieces = []
        for k in range(groups):
            start = k * rows
            for x in back[k]:
                pieces.append((start, x))
                start += x.shape[0]
        soft_labels = call(
            functools.partial(unpack_body, [start for start, _ in pieces]),
            jax.ShapeDtypeStruct((slot.shape[0], fine), BF),
            1 + len(pieces),
            HEAVY * slot.shape[0] * groups * rows * fine,
            HEAVY * groups * rows * fine * 2,
        )(slot, *[x for _, x in pieces])
        new_centroids = call(
            finish_body,
            jax.ShapeDtypeStruct(centroids.shape, F32),
            3,
            4 * per_device * fine * width,
            per_device * fine * width * 10,
        )(mine, mass, got)
        return soft_labels, new_centroids

    gathered = jnp.concatenate([blocks[k] for k in range(groups)], axis=0)
    shared = (first, held, gathered, slot, centroids)
    if halves == 1:
        return refine(range(groups), *shared)
    cases = [functools.partial(refine, c) for c in ((0, 3), (1, 2), range(groups))]
    return lax.switch(busy[0], cases, *shared)


def solution(mesh):
    placed = (
        P(("parts", "route"), None),
        P(("parts", "route")),
        P(("parts", "route"), None, None),
        P(("parts", "route")),
    )
    return jax.shard_map(
        shards,
        mesh=mesh,
        in_specs=placed,
        out_specs=(P(("parts", "route"), None), P(("parts", "route"), None, None)),
        check_vma=False,
    )
```
